512 devices in a mesh: din: 8 (over y), dout: 32 (over x, z), layer: 2 (over core).
Axes of the slice: x: 4, y: 8, z: 8, core: 2. Of those that a mesh axis runs over, the one named last changes fastest.
Arguments:
- acts: bfloat16 [2048, 8192], P(('layer', 'dout'), 'din'), parts along dimension 0, may hold values from -6 to 6
- grad_y: bfloat16 [2048, 8192], P(('layer', 'din'), 'dout'), parts along dimension 0, may hold values from -6 to 6
- w_base: bfloat16 [16384, 8192], P(('layer', 'din'), 'dout'), parts along dimension 0
- a_left: bfloat16 [16384, 64], P(('layer', 'din')), parts along dimension 0, may hold values from -0.0625 to 0.0625
- b_right: bfloat16 [128, 8192], P('layer', 'dout'), parts along dimension 0, may hold values from -0.75 to 0.75
- magnitude: float32 [16384], P(('layer', 'dout')), parts along dimension 0, may hold values from 0.5 to 2
Outputs:
- grad_acts: bfloat16 [2048, 8192], P(('layer', 'dout'), 'din'), parts along dimension 0
- grad_left: float32 [16384, 64], P(('layer', 'din', 'dout')), parts along dimension 0
- grad_right: float32 [128, 8192], P(('layer', 'din'), 'dout'), parts along dimension 0
- grad_mag: float32 [16384], P(('layer', 'dout')), parts along dimension 0
The draws below stay inside these ranges and needn't reach their ends.
There are 2 independent parts, one for each index of `layer`. The reference program is written for one: setup_inputs(seed, part) draws one part's arguments, and reference() takes and returns one part's arrays. A program takes and returns all parts, laid end to end along the dimension named above; each array names one. Nothing has to cross between parts.
All inputs are finite; a program needn't handle non-finite values.
Results may differ from the reference program's by a relative error of at most 0.023.
Values may be sent and summed in bfloat16 or wider, within the bound.
No kernel may reach another device: no remote copies, remote signals or barrier semaphores. Data moves between devices by JAX's collectives and lax.ppermute only.
A program may use at most 64 MiB of HBM per device.

```python
import math
import jax
import jax.numpy as jnp
from jax import lax

DIN = 8192
DOUT = 8192
RANK = 64
TOKENS = 1024
N_DOUT = 32


def draw_w_base(key, part):
    key = jax.random.fold_in(key, 11)
    key_base, key_cols = jax.random.split(key)
    rows = 1.0 + 2.0 * jnp.arange(DIN, dtype=jnp.float32) / max(DIN - 1, 1)
    cols = jnp.exp(jax.random.uniform(key_cols, (DOUT,), jnp.float32, 0.0, math.log(10.0)))
    base = jax.random.truncated_normal(key_base, -4.0, 4.0, (DIN, DOUT), jnp.float32)
    return (base * rows[:, None] * cols[None, :] / math.sqrt(DIN)).astype(jnp.bfloat16)


def block_levels(key, extent, shards, smallest, top_value):
    gain = 1.0
    for axis_at, blocks in shards:
        steps = jax.random.uniform(jax.random.fold_in(jax.random.fold_in(key, 6), axis_at), (blocks,), jnp.float32, smallest / len(shards), top_value / len(shards))
        gain = gain * jnp.repeat(jnp.exp(steps), extent[axis_at] // blocks).reshape((-1,) + (1,) * (len(extent) - 1 - axis_at))
    return gain


def gaussian(rng, extent, scale, limit, pieces=(), kind=jnp.bfloat16):
    values = scale * jax.random.normal(rng, extent, jnp.float32)
    if pieces:
        values = values * block_levels(rng, extent, pieces, -0.22, 0.18)
    return jnp.clip(values, -limit, limit).astype(kind)


def setup_inputs(seed: int = 0, part: int = 0) -> dict:
    key_list = jax.random.split(jax.random.key(seed), 7)
    part_keys = jax.random.split(jax.random.fold_in(key_list[6], part), 7)
    acts = gaussian(part_keys[0], (TOKENS, DIN), 1.0, 6.0, ((0, 32), (1, 8)))
    grad_y = gaussian(part_keys[1], (TOKENS, DOUT), 1.0, 6.0, ((0, 8), (1, 32)))
    w_base = draw_w_base(jax.random.fold_in(jax.random.fold_in(key_list[6], part), 71), part)
    a_left = gaussian(part_keys[3], (DIN, RANK), DIN ** -0.5, 0.0625, ((0, 8),))
    b_right = gaussian(part_keys[4], (RANK, DOUT), RANK ** -0.5, 0.75, ((1, 32),))
    magnitude = jnp.clip(jnp.exp(math.log(2.0) - 1.3862944 * jax.random.uniform(part_keys[5], (DOUT,), jnp.float32) ** block_levels(part_keys[5], (DOUT,), ((0, 32),), -0.2, 0.2)), 0.5, 2.0)
    return {"acts": acts, "grad_y": grad_y, "w_base": w_base, "a_left": a_left, "b_right": b_right, "magnitude": magnitude}


def reference(acts, grad_y, w_base, a_left, b_right, magnitude):
    merged = w_base.astype(jnp.float32) + jnp.dot(a_left, b_right, preferred_element_type=jnp.float32)
    merged_b = merged.astype(jnp.bfloat16)
    squares = lax.optimization_barrier(jnp.sum(merged * merged, axis=0))
    norms = jnp.sqrt(squares)
    outputs = jnp.dot(acts, merged_b, preferred_element_type=jnp.float32)
    stat = lax.optimization_barrier(jnp.sum(grad_y.astype(jnp.float32) * outputs, axis=0))
    grad_mag = stat / norms
    scale = magnitude / norms
    scaled = (grad_y.astype(jnp.float32) * scale[None, :]).astype(jnp.bfloat16)
    width = DOUT // N_DOUT

    def block_step(total, index):
        start = (index * width).astype(jnp.int32)
        rows = lax.dynamic_slice_in_dim(scaled, start, width, 1)
        cols = lax.dynamic_slice_in_dim(merged_b, start, width, 1)
        part = lax.dot_general(rows, cols, (((1,), (1,)), ((), ())), preferred_element_type=jnp.float32)
        rounded = lax.optimization_barrier(part.astype(jnp.bfloat16))
        return (total + rounded.astype(jnp.float32), None)
    total, unused = lax.scan(block_step, jnp.zeros((TOKENS, DIN), jnp.float32), jnp.arange(N_DOUT, dtype=jnp.int32))
    grad_acts = total.astype(jnp.bfloat16)
    products = lax.dot_general(acts, grad_y, (((0,), (0,)), ((), ())), preferred_element_type=jnp.float32)
    grad_merged = (products * scale[None, :]).astype(jnp.bfloat16)
    grad_left = lax.dot_general(grad_merged, b_right, (((1,), (1,)), ((), ())), preferred_element_type=jnp.float32)
    grad_right = lax.dot_general(a_left, grad_merged, (((0,), (0,)), ((), ())), preferred_element_type=jnp.float32)
    return (grad_acts, grad_left, grad_right, grad_mag)
```

```python
import jax
import jax.numpy as jnp
from jax import lax
from jax.sharding import Mesh, PartitionSpec as P

F32 = jnp.float32
BF16 = jnp.bfloat16


def spread(block, axis, count):
    return lax.all_to_all(
        jnp.broadcast_to(block[None], (count, *block.shape)), axis, 0, 0, tiled=True
    )


def local(acts, grad_y, w_base, a_left, b_right, magnitude):
    nx, ny, nz = 4, 8, 8
    rows, din = acts.shape
    width = grad_y.shape[1]
    rank = a_left.shape[1]
    tokens = rows * nz
    grads = spread(grad_y, "din", ny).reshape(-1, width)
    merged = w_base.astype(F32) + jnp.dot(a_left, b_right, preferred_element_type=F32)
    merged_b = merged.astype(BF16)
    square_part = jnp.sum(merged * merged, axis=0)
    squares = jnp.sum(spread(square_part[None], "din", ny), axis=(0, 1))
    wide = lax.all_gather(merged_b, "x")
    whole = spread(acts, "z", nz).reshape(tokens, din)
    scale = magnitude / jnp.sqrt(squares)
    scaled = (grads.astype(F32) * scale[None, :]).astype(BF16)
    low = lax.dot_general(
        scaled, b_right, (((1,), (1,)), ((), ())), preferred_element_type=F32
    ).astype(BF16)
    mine = lax.all_to_all(scaled.reshape(nx, tokens, width), "x", 0, 0, tiled=True)
    low_mine = lax.all_to_all(low.reshape(nx, tokens, rank), "x", 0, 0, tiled=True)
    part = sum(
        lax.dot_general(
            mine[k], wide[k], (((1,), (1,)), ((), ())), preferred_element_type=F32
        )
        for k in range(nx)
    ).astype(BF16)
    summed = jnp.sum(
        lax.all_to_all(part.reshape(nz, rows, din), "z", 0, 0, tiled=True).astype(F32),
        axis=0,
    ).astype(BF16)
    low_sum = jnp.sum(low_mine.astype(F32), axis=0).astype(BF16)
    left_part = lax.dot_general(
        whole, low_sum, (((0,), (0,)), ((), ())), preferred_element_type=F32
    ).astype(BF16)
    grad_left = jnp.sum(
        lax.all_to_all(
            left_part.reshape(nx * nz, -1, rank), ("x", "z"), 0, 0, tiled=True
        ).astype(F32),
        axis=0,
    )
    down = jnp.dot(whole, a_left, preferred_element_type=F32).astype(BF16)
    pieces = []
    for k in range(nx):
        outputs = jnp.dot(whole, wide[k], preferred_element_type=F32)
        stat = jnp.sum(mine[k].astype(F32) * outputs, axis=0)
        high = stat.astype(BF16)
        rest = (stat - high.astype(F32)).astype(BF16)
        right = lax.dot_general(
            down, mine[k], (((0,), (0,)), ((), ())), preferred_element_type=F32
        ).astype(BF16)
        tail = jnp.broadcast_to(jnp.stack([high, rest])[None], (ny, 2, width))
        pieces.append(
            jnp.concatenate([right.reshape(ny, rank // ny, width), tail], axis=1)
        )
    packed = jnp.stack(pieces, axis=1).reshape(ny * nx, rank // ny + 2, width)
    got = jnp.sum(
        lax.all_to_all(packed, ("din", "x"), 0, 0, tiled=True).astype(F32), axis=0
    )
    grad_right = got[: rank // ny]
    grad_mag = (got[rank // ny] + got[rank // ny + 1]) / magnitude
    return (summed, grad_left, grad_right, grad_mag)


def solution(mesh):
    fine = Mesh(mesh.devices.reshape(8, 4, 8, 2), ("din", "x", "z", "layer"))
    return jax.shard_map(
        local,
        mesh=fine,
        in_specs=(
            P(("layer", "x", "z"), "din"),
            P(("layer", "din"), ("x", "z")),
            P(("layer", "din"), ("x", "z")),
            P(("layer", "din"), None),
            P("layer", ("x", "z")),
            P(("layer", "x", "z")),
        ),
        out_specs=(
            P(("layer", "x", "z"), "din"),
            P(("layer", "din", "x", "z"), None),
            P(("layer", "din"), ("x", "z")),
            P(("layer", "x", "z")),
        ),
        check_vma=False,
    )
```

```python
import jax
import jax.numpy as jnp
from jax import lax
from jax.experimental import pallas as pl
from jax.experimental.pallas import tpu as pltpu
from jax.sharding import Mesh, PartitionSpec as P

F32 = jnp.float32
BF16 = jnp.bfloat16
NX, NY, NZ = 4, 8, 8
NT = (((1,), (1,)), ((), ()))
TN = (((0,), (0,)), ((), ()))
VMEM = pl.BlockSpec(memory_space=pltpu.VMEM)
SMEM = pl.BlockSpec(memory_space=pltpu.SMEM)
LIMIT = 48 * 1024 * 1024
HOPS = (0, 1, 3, 2)


def dot(a, b, dims):
    return lax.dot_general(a, b, dims, preferred_element_type=F32)


def call(body, outs, flops, *args):
    moved = sum(a.size * a.dtype.itemsize for a in args)
    moved += sum(o.size * o.dtype.itemsize for o in outs)
    return pl.pallas_call(
        body,
        out_shape=outs,
        in_specs=[SMEM if a.dtype == jnp.int32 else VMEM for a in args],
        out_specs=[VMEM] * len(outs),
        compiler_params=pltpu.CompilerParams(vmem_limit_bytes=LIMIT),
        cost_estimate=pl.CostEstimate(
            flops=flops, bytes_accessed=moved, transcendentals=0
        ),
    )(*args)


def shape(dims, dtype=BF16):
    return jax.ShapeDtypeStruct(dims, dtype)


def two_rows(value, width):
    high = value.astype(BF16).astype(F32)
    row = lax.broadcasted_iota(jnp.int32, (16, width), 0)
    return jnp.where(row == 0, high, jnp.where(row == 1, value - high, 0.0)).astype(BF16)


def merge_body(w_ref, at_ref, b_ref, g_ref, wide_ref, pay_ref):
    din, width = w_ref.shape
    rank = b_ref.shape[0]
    tokens = g_ref.shape[0]
    total = jnp.zeros((1, width), F32)
    step = 256
    for i in range(0, din, step):
        merged = w_ref[pl.ds(i, step), :].astype(F32) + dot(
            at_ref[:, pl.ds(i, step)], b_ref[...], TN
        )
        total += jnp.sum(merged * merged, axis=0, keepdims=True)
        wide_ref[pl.ds(i, step), :] = merged.astype(BF16)
    wide_ref[pl.ds(din, rank), :] = b_ref[...]
    tail = two_rows(total, width)
    for y in range(NY):
        pay_ref[y, pl.ds(0, tokens), :] = g_ref[...]
        pay_ref[y, pl.ds(tokens, 16), :] = tail


def scale_body(x_ref, got_ref, mag_ref, *outs):
    tokens = got_ref.shape[1] - 16
    width = got_ref.shape[2]
    squares = jnp.zeros((16, width), F32)
    for y in range(NY):
        squares += got_ref[y, pl.ds(tokens, 16), :].astype(F32)
    squares = jnp.sum(squares, axis=0, keepdims=True)
    scale = mag_ref[...] / jnp.sqrt(squares)
    half = NY // NX
    for hop, out in zip(HOPS, outs):
        block = lax.rem(x_ref[0] + hop, NX)
        for h in range(half):
            out[pl.ds(h * tokens, tokens), :] = (
                got_ref[block * half + h, pl.ds(0, tokens), :].astype(F32) * scale
            ).astype(BF16)


def source(x_ref, k):
    return lax.rem(x_ref[0] + NX - HOPS[k], NX)


def acts_body(x_ref, s0, s1, s2, s3, wide_ref, whole_ref, out_ref):
    blocks = (s0, s1, s2, s3)
    tokens, din = whole_ref.shape
    rank = wide_ref.shape[1] - din
    step = 256
    for i in range(0, din, step):
        total = sum(
            dot(s[...], wide_ref[source(x_ref, k), pl.ds(i, step), :], NT)
            for k, s in enumerate(blocks)
        )
        out_ref[:, pl.ds(i, step)] = total.astype(BF16)
    low = jnp.zeros((tokens, NX * rank), F32)
    for k, s in enumerate(blocks):
        b = wide_ref[source(x_ref, k), pl.ds(din, rank), :]
        low += dot(s[...], jnp.concatenate([b] * NX, axis=0), NT)
    low = low.astype(BF16)
    lane = lax.broadcasted_iota(jnp.int32, low.shape, 1)
    left = jnp.zeros((din // NX, NX * rank), F32)
    for q in range(NX):
        here = (lane >= q * rank) & (lane < (q + 1) * rank)
        left += dot(
            whole_ref[:, pl.ds(q * (din // NX), din // NX)],
            jnp.where(here, low, jnp.zeros_like(low)),
            TN,
        )
    out_ref[:, pl.ds(din, NX * rank)] = left.astype(BF16)


def stat_body(x_ref, s0, s1, s2, s3, wide_ref, whole_ref, at_ref, *outs):
    din = whole_ref.shape[1]
    rank = at_ref.shape[0]
    down = dot(whole_ref[...], at_ref[...], NT).astype(BF16)
    for k, (s, out) in enumerate(zip((s0, s1, s2, s3), outs)):
        outputs = lax.dot_general(
            whole_ref[...],
            wide_ref[source(x_ref, k), pl.ds(0, din), :],
            (((1,), (0,)), ((), ())),
            preferred_element_type=F32,
        )
        stat = jnp.sum(s[...].astype(F32) * outputs, axis=0, keepdims=True)
        out[pl.ds(0, rank), :] = dot(down, s[...], TN).astype(BF16)
        out[pl.ds(rank, 16), :] = two_rows(stat, stat.shape[1])


def meet_body(r0, r1, r2, r3, pay_ref):
    rows, width = r0.shape
    total = sum(r[...].astype(F32) for r in (r0, r1, r2, r3))
    stat = jnp.sum(total[rows - 16 :], axis=0, keepdims=True)
    tail = two_rows(stat, width)
    each = (rows - 16) // NY
    for y in range(NY):
        pay_ref[y, :, :] = jnp.concatenate(
            [
                total[y * each : (y + 1) * each],
                tail.astype(F32)[:8],
            ],
            axis=0,
        ).astype(BF16)


def sum_body(got_ref, acts_ref, left_ref):
    din = acts_ref.shape[1]
    total = sum(got_ref[z].astype(F32) for z in range(NZ))
    acts_ref[...] = total[:, :din].astype(BF16)
    left_ref[...] = total[:, din:].astype(BF16)


def shift(block, hop):
    return lax.ppermute(block, "x", [(i, (i + hop) % NX) for i in range(NX)])


def local(acts, grad_y, w_base, a_left, b_right, magnitude):
    rows, din = acts.shape
    width = grad_y.shape[1]
    rank = a_left.shape[1]
    tokens = rows * NZ
    spot = lax.axis_index("x").astype(jnp.int32).reshape(1)
    a_turned = a_left.T
    packed, pay = call(
        merge_body,
        [shape((din + rank, width)), shape((NY, grad_y.shape[0] + 16, width))],
        2 * din * width * rank,
        w_base, a_turned, b_right, grad_y,
    )
    wide = lax.all_gather(packed, "x")
    got = lax.all_to_all(pay, "din", 0, 0, tiled=True)
    scaled = call(
        scale_body,
        [shape((tokens, width))] * NX,
        4 * tokens * width * NX,
        spot, got, magnitude.reshape(1, width),
    )
    blocks = [scaled[0]] + [shift(scaled[k], HOPS[k]) for k in range(1, NX)]
    whole = lax.all_to_all(
        jnp.broadcast_to(acts[None], (NZ, rows, din)), "z", 0, 0, tiled=True
    ).reshape(tokens, din)
    (part,) = call(
        acts_body,
        [shape((tokens, din + NX * rank))],
        2 * tokens * din * width * NX,
        spot, *blocks, wide, whole,
    )
    back = lax.all_to_all(
        part.reshape(NZ, rows, din + NX * rank), "z", 0, 0, tiled=True
    )
    sides = call(
        stat_body,
        [shape((rank + 16, width))] * NX,
        2 * tokens * din * width * NX,
        spot, *blocks, wide, whole, a_turned,
    )
    met = [sides[0]] + [shift(sides[k], NX - HOPS[k]) for k in range(1, NX)]
    (pay,) = call(meet_body, [shape((NY, 16, width))], 0, *met)
    summed, left = call(
        sum_body, [shape((rows, din)), shape((rows, NX * rank))], 0, back
    )
    right = jnp.sum(
        lax.all_to_all(pay, "din", 0, 0, tiled=True).astype(F32), axis=0
    )
    lefts = left.astype(F32)
    for hop in (1, 3, 2):
        lefts += shift(left, hop).astype(F32)
    grad_left = lax.dynamic_slice_in_dim(lefts, spot[0] * rank, rank, 1)
    each = rank // NY
    grad_mag = (right[each] + right[each + 1]) / magnitude
    return (summed, grad_left, right[:each], grad_mag)


def solution(mesh):
    fine = Mesh(mesh.devices.reshape(NY, NX, NZ, 2), ("din", "x", "z", "layer"))
    return jax.shard_map(
        local,
        mesh=fine,
        in_specs=(
            P(("layer", "x", "z"), "din"),
            P(("layer", "din"), ("x", "z")),
            P(("layer", "din"), ("x", "z")),
            P(("layer", "din"), None),
            P("layer", ("x", "z")),
            P(("layer", "x", "z")),
        ),
        out_specs=(
            P(("layer", "x", "z"), "din"),
            P(("layer", "din", "x", "z"), None),
            P(("layer", "din"), ("x", "z")),
            P(("layer", "x", "z")),
        ),
        check_vma=False,
    )
```

```python
import jax
import jax.numpy as jnp
from jax import lax
from jax.experimental import pallas as pl
from jax.experimental.pallas import tpu as pltpu
from jax.sharding import Mesh, PartitionSpec as P

F32 = jnp.float32
BF16 = jnp.bfloat16
NX, NY, NZ = 4, 8, 8
NT = (((1,), (1,)), ((), ()))
TN = (((0,), (0,)), ((), ()))
NN = (((1,), (0,)), ((), ()))
VMEM = pl.BlockSpec(memory_space=pltpu.VMEM)
SMEM = pl.BlockSpec(memory_space=pltpu.SMEM)
HBM = pl.BlockSpec(memory_space=pltpu.HBM)
MIB = 1024 * 1024
STEP = 256
HOPS = (0, 1, 3, 2)


def dot(a, b, dims):
    return lax.dot_general(a, b, dims, preferred_element_type=F32)


def shape(dims, dtype=BF16):
    return jax.ShapeDtypeStruct(dims, dtype)


def call(body, outs, flops, *args, far=(), scratch=(), out_specs=None, limit=16):
    moved = sum(a.size * a.dtype.itemsize for a in args)
    moved += sum(o.size * o.dtype.itemsize for o in outs)
    specs = [
        HBM if i in far else SMEM if a.dtype == jnp.int32 else VMEM
        for i, a in enumerate(args)
    ]
    return pl.pallas_call(
        body,
        out_shape=outs,
        in_specs=specs,
        out_specs=out_specs or [VMEM] * len(outs),
        scratch_shapes=scratch,
        compiler_params=pltpu.CompilerParams(vmem_limit_bytes=limit * MIB),
        cost_estimate=pl.CostEstimate(
            flops=flops, bytes_accessed=moved, transcendentals=0
        ),
    )(*args)


def fetch(pairs, sems):
    copies = [
        pltpu.make_async_copy(src, dst, sems.at[i]) for i, (src, dst) in enumerate(pairs)
    ]
    for copy in copies:
        copy.start()
    return copies


def two_rows(value, width):
    high = value.astype(BF16).astype(F32)
    row = lax.broadcasted_iota(jnp.int32, (16, width), 0)
    return jnp.where(row == 0, high, jnp.where(row == 1, value - high, 0.0)).astype(BF16)


def merge_body(w_hbm, at_hbm, b_hbm, g_hbm, pay_ref, w_ref, at_ref, b_ref, g_ref, sems):
    copies = fetch(
        ((w_hbm, w_ref), (at_hbm, at_ref), (b_hbm, b_ref), (g_hbm, g_ref)), sems
    )
    for copy in copies:
        copy.wait()
    din, width = w_ref.shape
    tokens = g_ref.shape[0]
    total = jnp.zeros((1, width), F32)
    for i in range(0, din, STEP):
        merged = w_ref[pl.ds(i, STEP), :].astype(F32) + dot(
            at_ref[:, pl.ds(i, STEP)], b_ref[...], TN
        )
        total += jnp.sum(merged * merged, axis=0, keepdims=True)
    tail = two_rows(total, width)
    for y in range(NY):
        pay_ref[y, pl.ds(0, tokens), :] = g_ref[...]
        pay_ref[y, pl.ds(tokens, 16), :] = tail


def scale_body(x_ref, got_ref, mag_ref, b_ref, *outs):
    tokens = got_ref.shape[1] - 16
    width = got_ref.shape[2]
    squares = jnp.zeros((16, width), F32)
    for y in range(NY):
        squares += got_ref[y, pl.ds(tokens, 16), :].astype(F32)
    squares = jnp.sum(squares, axis=0, keepdims=True)
    scale = mag_ref[...] / jnp.sqrt(squares)
    half = NY // NX
    for hop, out in zip(HOPS, outs):
        block = lax.rem(x_ref[0] + hop, NX)
        for h in range(half):
            out[pl.ds(h * tokens, tokens), :] = (
                got_ref[block * half + h, pl.ds(0, tokens), :].astype(F32) * scale
            ).astype(BF16)
        out[pl.ds(half * tokens, b_ref.shape[0]), :] = b_ref[...]


def source(x_ref, k):
    return lax.rem(x_ref[0] + NX - HOPS[k], NX)


def acts_body(
    x_ref, s0, s1, s2, s3, wide_hbm, at, whole, out_hbm, wide, out, lefts, sems, out_sems
):
    blocks = (s0, s1, s2, s3)
    tokens, din = whole.shape
    rank = at.shape[0]
    steps = din // STEP
    copies = fetch(
        [
            (
                wide_hbm.at[source(x_ref, k), pl.ds(i * STEP, STEP)],
                wide.at[k, pl.ds(i * STEP, STEP)],
            )
            for i in range(steps)
            for k in range(NX)
        ],
        sems,
    )
    low = jnp.zeros((tokens, NX * rank), F32)
    for s in blocks:
        b = s[pl.ds(tokens, rank), :]
        low += dot(s[pl.ds(0, tokens), :], jnp.concatenate([b] * NX, axis=0), NT)
    low = low.astype(BF16)
    sends = []

    def send(start, count):
        sends.append(
            pltpu.make_async_copy(
                out.at[:, pl.ds(start, count)],
                out_hbm.at[:, pl.ds(start, count)],
                out_sems.at[len(sends)],
            )
        )
        sends[-1].start()

    group = lax.div(lax.broadcasted_iota(jnp.int32, (8, NX * rank), 1), rank)
    each = din // NX
    rows = each // NZ
    for q in range(NX):
        left = dot(whole[:, pl.ds(q * each, each)], low, TN)
        for z in range(NZ):
            piece = jnp.zeros((8, NX * rank), F32)
            for g in range(rows // 8):
                first = z * rows + g * 8
                piece += jnp.where(group == g, left[first : first + 8], 0.0)
            lefts[pl.ds(z * rows + q * 8, 8), :] = piece
    out[:, pl.ds(din, NX * rank)] = lefts[...].astype(BF16)
    send(din, NX * rank)
    for i in range(steps):
        total = dot(low[:, :rank], at[:, pl.ds(i * STEP, STEP)], NN)
        for k, s in enumerate(blocks):
            copies[i * NX + k].wait()
            total += dot(s[pl.ds(0, tokens), :], wide[k, pl.ds(i * STEP, STEP), :], NT)
        out[:, pl.ds(i * STEP, STEP)] = total.astype(BF16)
        send(i * STEP, STEP)
    for copy in sends:
        copy.wait()


def stat_body(x_ref, s0, s1, s2, s3, wide_hbm, at, whole, *rest):
    outs, (wide, sems) = rest[:NX], rest[NX:]
    copies = fetch(
        [(wide_hbm.at[source(x_ref, k)], wide.at[k]) for k in range(NX)], sems
    )
    rank = at.shape[0]
    tokens = whole.shape[0]
    down = dot(whole[...], at[...], NT).astype(BF16)
    for k, (s, out) in enumerate(zip((s0, s1, s2, s3), outs)):
        scaled = s[pl.ds(0, tokens), :]
        out[pl.ds(0, rank), :] = dot(down, scaled, TN).astype(BF16)
        copies[k].wait()
        outputs = dot(whole[...], wide[k], NN) + dot(down, s[pl.ds(tokens, rank), :], NN)
        stat = jnp.sum(scaled.astype(F32) * outputs, axis=0, keepdims=True)
        out[pl.ds(rank, 16), :] = two_rows(stat, stat.shape[1])


def meet_body(r0, r1, r2, r3, pay_ref):
    rows, width = r0.shape
    total = sum(r[...].astype(F32) for r in (r0, r1, r2, r3))
    stat = jnp.sum(total[rows - 16 :], axis=0, keepdims=True)
    tail = two_rows(stat, width).astype(F32)[:8]
    each = (rows - 16) // NY
    for y in range(NY):
        pay_ref[y, :, :] = jnp.concatenate(
            [total[y * each : (y + 1) * each], tail], axis=0
        ).astype(BF16)


def sum_body(x_ref, got_ref, acts_ref, keep_ref, send_ref, lefts):
    din = acts_ref.shape[1]
    total = sum(got_ref[z].astype(F32) for z in range(NZ))
    acts_ref[...] = total[:, :din].astype(BF16)
    lefts[...] = total[:, din:]

    def block(mask):
        x = jnp.bitwise_xor(x_ref[0], mask)
        return lefts[pl.ds(pl.multiple_of(x * 8, 8), 8), :]

    keep_ref[...] = jnp.concatenate([block(0), block(3)], axis=0)
    send_ref[...] = jnp.concatenate([block(1), block(2)], axis=0).astype(BF16)


def pair_body(keep_ref, got_ref, own_ref, send_ref):
    total = keep_ref[...] + got_ref[...].astype(F32)
    own_ref[...] = total[:8]
    send_ref[...] = jnp.concatenate([total[8:], total[8:]], axis=0).astype(BF16)


def last_body(own_ref, more_ref, got_ref, mag_ref, left_ref, right_ref, mag_out):
    total = sum(got_ref[y].astype(F32) for y in range(NY))
    right_ref[...] = total[:8]
    mag_out[...] = (total[8:9] + total[9:10]) / mag_ref[...]
    left = own_ref[...] + more_ref[...].astype(F32)[:8]
    rank = left_ref.shape[1]
    for g in range(left_ref.shape[0] // 8):
        left_ref[pl.ds(g * 8, 8), :] = left[:, g * rank : (g + 1) * rank]


def shift(block, hop):
    return lax.ppermute(block, "x", [(i, (i + hop) % NX) for i in range(NX)])


def swap(block, mask):
    return lax.ppermute(block, "x", [(i, i ^ mask) for i in range(NX)])


def after(value, *others):
    return lax.optimization_barrier((value, *others))[0]


def local(acts, grad_y, w_base, a_left, b_right, magnitude):
    rows, din = acts.shape
    width = grad_y.shape[1]
    rank = a_left.shape[1]
    tokens = rows * NZ
    wider = din + NX * rank
    spot = lax.axis_index("x").astype(jnp.int32).reshape(1)
    mags = magnitude.reshape(1, width)
    a_turned = a_left.T
    wide = lax.all_gather(w_base, "x")
    parts = (w_base, a_turned, b_right, grad_y)
    (pay,) = call(
        merge_body,
        [shape((NY, grad_y.shape[0] + 16, width))],
        2 * din * width * rank,
        *parts,
        far=(0, 1, 2, 3),
        scratch=[pltpu.VMEM(p.shape, p.dtype) for p in parts]
        + [pltpu.SemaphoreType.DMA((4,))],
        limit=60,
    )
    got = lax.all_to_all(pay, "din", 0, 0, tiled=True)
    scaled = call(
        scale_body,
        [shape((tokens + rank, width))] * NX,
        4 * tokens * width * NX,
        spot, got, mags, b_right,
    )
    blocks = [scaled[0]] + [shift(scaled[k], HOPS[k]) for k in range(1, NX)]
    whole = lax.all_to_all(
        after(jnp.broadcast_to(acts[None], (NZ, rows, din)), got), "z", 0, 0, tiled=True
    ).reshape(tokens, din)
    room = pltpu.VMEM((NX, din, width), BF16)
    (part,) = call(
        acts_body,
        [shape((tokens, wider))],
        2 * tokens * din * width * NX,
        spot, *blocks, wide, a_turned, whole,
        far=(5,),
        out_specs=[HBM],
        scratch=[
            room,
            pltpu.VMEM((tokens, wider), BF16),
            pltpu.VMEM((tokens, NX * rank), F32),
            pltpu.SemaphoreType.DMA((NX * (din // STEP),)),
            pltpu.SemaphoreType.DMA((1 + din // STEP,)),
        ],
        limit=58,
    )
    back = lax.all_to_all(part.reshape(NZ, rows, wider), "z", 0, 0, tiled=True)
    sides = call(
        stat_body,
        [shape((rank + 16, width))] * NX,
        2 * tokens * din * width * NX,
        after(spot, part), *blocks, wide, a_turned, whole,
        far=(5,),
        scratch=[room, pltpu.SemaphoreType.DMA((NX,))],
        limit=58,
    )
    met = [sides[0]] + [shift(sides[k], NX - HOPS[k]) for k in range(1, NX)]
    (pay,) = call(meet_body, [shape((NY, 16, width))], 0, *met)
    back, pay = lax.optimization_barrier((back, pay))
    right = lax.all_to_all(pay, "din", 0, 0, tiled=True)
    summed, keep, send = call(
        sum_body,
        [shape((rows, din)), shape((16, width), F32), shape((16, width))],
        0,
        spot, back,
        scratch=[pltpu.VMEM((rows, NX * rank), F32)],
    )
    own, send = call(
        pair_body, [shape((8, width), F32), shape((16, width))], 0, keep, swap(send, 1)
    )
    grad_left, grad_right, grad_mag = call(
        last_body,
        [shape((rows, rank), F32), shape((rank // NY, width), F32), shape((1, width), F32)],
        0,
        own, swap(send, 3), right, mags,
    )
    return (summed, grad_left, grad_right, grad_mag.reshape(width))


def solution(mesh):
    fine = Mesh(mesh.devices.reshape(NY, NX, NZ, 2), ("din", "x", "z", "layer"))
    return jax.shard_map(
        local,
        mesh=fine,
        in_specs=(
            P(("layer", "x", "z"), "din"),
            P(("layer", "din"), ("x", "z")),
            P(("layer", "din"), ("x", "z")),
            P(("layer", "din"), None),
            P("layer", ("x", "z")),
            P(("layer", "x", "z")),
        ),
        out_specs=(
            P(("layer", "x", "z"), "din"),
            P(("layer", "din", "x", "z"), None),
            P(("layer", "din"), ("x", "z")),
            P(("layer", "x", "z")),
        ),
        check_vma=False,
    )
```

```python
import jax
import jax.numpy as jnp
from jax import lax
from jax.experimental import pallas as pl
from jax.experimental.pallas import tpu as pltpu
from jax.sharding import Mesh, PartitionSpec as P

F32 = jnp.float32
BF16 = jnp.bfloat16
NX, NY, NZ = 4, 8, 8
NT = (((1,), (1,)), ((), ()))
TN = (((0,), (0,)), ((), ()))
NN = (((1,), (0,)), ((), ()))
VMEM = pl.BlockSpec(memory_space=pltpu.VMEM)
SMEM = pl.BlockSpec(memory_space=pltpu.SMEM)
HBM = pl.BlockSpec(memory_space=pltpu.HBM)
MIB = 1024 * 1024
STEP = 256
HOPS = (0, 1, 3, 2)


def dot(a, b, dims):
    return lax.dot_general(a, b, dims, preferred_element_type=F32)


def shape(dims, dtype=BF16):
    return jax.ShapeDtypeStruct(dims, dtype)


def call(body, outs, flops, *args, far=(), scratch=(), out_specs=None, limit=16):
    moved = sum(a.size * a.dtype.itemsize for a in args)
    moved += sum(o.size * o.dtype.itemsize for o in outs)
    specs = [
        HBM if i in far else SMEM if a.dtype == jnp.int32 else VMEM
        for i, a in enumerate(args)
    ]
    return pl.pallas_call(
        body,
        out_shape=outs,
        in_specs=specs,
        out_specs=out_specs or [VMEM] * len(outs),
        scratch_shapes=scratch,
        compiler_params=pltpu.CompilerParams(vmem_limit_bytes=limit * MIB),
        cost_estimate=pl.CostEstimate(
            flops=flops, bytes_accessed=moved, transcendentals=0
        ),
    )(*args)


def fetch(pairs, sems):
    copies = [
        pltpu.make_async_copy(src, dst, sems.at[i]) for i, (src, dst) in enumerate(pairs)
    ]
    for copy in copies:
        copy.start()
    return copies


def two_rows(value, width):
    high = value.astype(BF16).astype(F32)
    row = lax.broadcasted_iota(jnp.int32, (16, width), 0)
    return jnp.where(row == 0, high, jnp.where(row == 1, value - high, 0.0)).astype(BF16)


def merge_body(
    w_hbm, at_hbm, b_hbm, g_hbm, acts_hbm, pay_ref, many_hbm, w_ref, at_ref, b_ref, g_ref, acts_ref, sems, more
):
    copies = fetch(
        (
            (acts_hbm, acts_ref),
            (w_hbm, w_ref),
            (at_hbm, at_ref),
            (b_hbm, b_ref),
            (g_hbm, g_ref),
        ),
        sems,
    )
    copies[0].wait()
    repeats = fetch([(acts_ref, many_hbm.at[z]) for z in range(NZ)], more)
    for copy in copies[1:]:
        copy.wait()
    din, width = w_ref.shape
    tokens = g_ref.shape[0]
    total = jnp.zeros((1, width), F32)
    for i in range(0, din, STEP):
        merged = w_ref[pl.ds(i, STEP), :].astype(F32) + dot(
            at_ref[:, pl.ds(i, STEP)], b_ref[...], TN
        )
        total += jnp.sum(merged * merged, axis=0, keepdims=True)
    tail = two_rows(total, width)
    for y in range(NY):
        pay_ref[y, pl.ds(0, tokens), :] = g_ref[...]
        pay_ref[y, pl.ds(tokens, 16), :] = tail
    for copy in repeats:
        copy.wait()


def scale_body(x_ref, got_ref, mag_ref, b_ref, *outs):
    tokens = got_ref.shape[1] - 16
    width = got_ref.shape[2]
    squares = jnp.zeros((16, width), F32)
    for y in range(NY):
        squares += got_ref[y, pl.ds(tokens, 16), :].astype(F32)
    squares = jnp.sum(squares, axis=0, keepdims=True)
    scale = mag_ref[...] / jnp.sqrt(squares)
    half = NY // NX
    for hop, out in zip(HOPS, outs):
        block = lax.rem(x_ref[0] + hop, NX)
        for h in range(half):
            out[pl.ds(h * tokens, tokens), :] = (
                got_ref[block * half + h, pl.ds(0, tokens), :].astype(F32) * scale
            ).astype(BF16)
        out[pl.ds(half * tokens, b_ref.shape[0]), :] = b_ref[...]


def source(x_ref, k):
    return lax.rem(x_ref[0] + NX - HOPS[k], NX)


def acts_body(
    x_ref, s0, s1, s2, s3, wide, at, whole, out_hbm, out, lefts, out_sems
):
    blocks = (s0, s1, s2, s3)
    tokens, din = whole.shape
    rank = at.shape[0]
    steps = din // STEP
    place = [source(x_ref, k) for k in range(NX)]
    low = jnp.zeros((tokens, NX * rank), F32)
    for s in blocks:
        b = s[pl.ds(tokens, rank), :]
        low += dot(s[pl.ds(0, tokens), :], jnp.concatenate([b] * NX, axis=0), NT)
    low = low.astype(BF16)
    sends = []

    def send(start, count):
        sends.append(
            pltpu.make_async_copy(
                out.at[:, pl.ds(start, count)],
                out_hbm.at[:, pl.ds(start, count)],
                out_sems.at[len(sends)],
            )
        )
        sends[-1].start()

    group = lax.div(lax.broadcasted_iota(jnp.int32, (8, NX * rank), 1), rank)
    each = din // NX
    rows = each // NZ
    for q in range(NX):
        left = dot(whole[:, pl.ds(q * each, each)], low, TN)
        for z in range(NZ):
            piece = jnp.zeros((8, NX * rank), F32)
            for g in range(rows // 8):
                first = z * rows + g * 8
                piece += jnp.where(group == g, left[first : first + 8], 0.0)
            lefts[pl.ds(z * rows + q * 8, 8), :] = piece
    out[:, pl.ds(din, NX * rank)] = lefts[...].astype(BF16)
    send(din, NX * rank)
    for i in range(steps):
        total = dot(low[:, :rank], at[:, pl.ds(i * STEP, STEP)], NN)
        for k, s in enumerate(blocks):
            total += dot(
                s[pl.ds(0, tokens), :], wide[place[k], pl.ds(i * STEP, STEP), :], NT
            )
        out[:, pl.ds(i * STEP, STEP)] = total.astype(BF16)
        send(i * STEP, STEP)
    for copy in sends:
        copy.wait()


def stat_body(x_ref, s0, s1, s2, s3, wide, at, whole, *outs):
    rank = at.shape[0]
    tokens = whole.shape[0]
    down = dot(whole[...], at[...], NT).astype(BF16)
    for k, (s, out) in enumerate(zip((s0, s1, s2, s3), outs)):
        scaled = s[pl.ds(0, tokens), :]
        out[pl.ds(0, rank), :] = dot(down, scaled, TN).astype(BF16)
        outputs = dot(whole[...], wide[source(x_ref, k)], NN) + dot(down, s[pl.ds(tokens, rank), :], NN)
        stat = jnp.sum(scaled.astype(F32) * outputs, axis=0, keepdims=True)
        out[pl.ds(rank, 16), :] = two_rows(stat, stat.shape[1])


def meet_body(r0, r1, r2, r3, pay_ref):
    rows, width = r0.shape
    total = sum(r[...].astype(F32) for r in (r0, r1, r2, r3))
    stat = jnp.sum(total[rows - 16 :], axis=0, keepdims=True)
    tail = two_rows(stat, width).astype(F32)[:8]
    each = (rows - 16) // NY
    for y in range(NY):
        pay_ref[y, :, :] = jnp.concatenate(
            [total[y * each : (y + 1) * each], tail], axis=0
        ).astype(BF16)


def sum_body(x_ref, got_ref, acts_ref, keep_ref, send_ref, lefts):
    din = acts_ref.shape[1]
    total = sum(got_ref[z].astype(F32) for z in range(NZ))
    acts_ref[...] = total[:, :din].astype(BF16)
    lefts[...] = total[:, din:]

    def block(mask):
        x = jnp.bitwise_xor(x_ref[0], mask)
        return lefts[pl.ds(pl.multiple_of(x * 8, 8), 8), :]

    keep_ref[...] = jnp.concatenate([block(0), block(3)], axis=0)
    send_ref[...] = jnp.concatenate([block(1), block(2)], axis=0).astype(BF16)


def pair_body(keep_ref, got_ref, own_ref, send_ref):
    total = keep_ref[...] + got_ref[...].astype(F32)
    own_ref[...] = total[:8]
    send_ref[...] = jnp.concatenate([total[8:], total[8:]], axis=0).astype(BF16)


def last_body(own_ref, more_ref, got_ref, mag_ref, left_ref, right_ref, mag_out):
    total = sum(got_ref[y].astype(F32) for y in range(NY))
    right_ref[...] = total[:8]
    mag_out[...] = (total[8:9] + total[9:10]) / mag_ref[...]
    left = own_ref[...] + more_ref[...].astype(F32)[:8]
    rank = left_ref.shape[1]
    for g in range(left_ref.shape[0] // 8):
        left_ref[pl.ds(g * 8, 8), :] = left[:, g * rank : (g + 1) * rank]


def shift(block, hop):
    return lax.ppermute(block, "x", [(i, (i + hop) % NX) for i in range(NX)])


def swap(block, mask):
    return lax.ppermute(block, "x", [(i, i ^ mask) for i in range(NX)])


def after(value, *others):
    return lax.optimization_barrier((value, *others))[0]


def local(acts, grad_y, w_base, a_left, b_right, magnitude):
    rows, din = acts.shape
    width = grad_y.shape[1]
    rank = a_left.shape[1]
    tokens = rows * NZ
    wider = din + NX * rank
    spot = lax.axis_index("x").astype(jnp.int32).reshape(1)
    mags = magnitude.reshape(1, width)
    a_turned = a_left.T
    wide = lax.all_gather(w_base, "x")
    parts = (w_base, a_turned, b_right, grad_y)
    pay, many = call(
        merge_body,
        [shape((NY, grad_y.shape[0] + 16, width)), shape((NZ, rows, din))],
        2 * din * width * rank,
        *parts, acts,
        far=(0, 1, 2, 3, 4),
        out_specs=[VMEM, HBM],
        scratch=[pltpu.VMEM(p.shape, p.dtype) for p in (*parts, acts)]
        + [pltpu.SemaphoreType.DMA((5,)), pltpu.SemaphoreType.DMA((NZ,))],
        limit=60,
    )
    got = lax.all_to_all(pay, "din", 0, 0, tiled=True)
    scaled = call(
        scale_body,
        [shape((tokens + rank, width))] * NX,
        4 * tokens * width * NX,
        spot, got, mags, b_right,
    )
    blocks = [scaled[0]] + [shift(scaled[k], HOPS[k]) for k in range(1, NX)]
    whole = lax.all_to_all(after(many, got), "z", 0, 0, tiled=True).reshape(tokens, din)
    (part,) = call(
        acts_body,
        [shape((tokens, wider))],
        2 * tokens * din * width * NX,
        spot, *blocks, wide, a_turned, whole,
        out_specs=[HBM],
        scratch=[
            pltpu.VMEM((tokens, wider), BF16),
            pltpu.VMEM((tokens, NX * rank), F32),
            pltpu.SemaphoreType.DMA((1 + din // STEP,)),
        ],
    )
    back = lax.all_to_all(part.reshape(NZ, rows, wider), "z", 0, 0, tiled=True)
    sides = call(
        stat_body,
        [shape((rank + 16, width))] * NX,
        2 * tokens * din * width * NX,
        after(spot, part), *blocks, wide, a_turned, whole,
    )
    met = [sides[0]] + [shift(sides[k], NX - HOPS[k]) for k in range(1, NX)]
    summed, keep, send = call(
        sum_body,
        [shape((rows, din)), shape((16, width), F32), shape((16, width))],
        0,
        spot, back,
        scratch=[pltpu.VMEM((rows, NX * rank), F32)],
    )
    more = swap(send, 1)
    (pay,) = call(meet_body, [shape((NY, 16, width))], 0, after(met[0], more), *met[1:])
    right = lax.all_to_all(pay, "din", 0, 0, tiled=True)
    own, send = call(
        pair_body, [shape((8, width), F32), shape((16, width))], 0, keep, more
    )
    grad_left, grad_right, grad_mag = call(
        last_body,
        [shape((rows, rank), F32), shape((rank // NY, width), F32), shape((1, width), F32)],
        0,
        own, swap(send, 3), right, mags,
    )
    return (summed, grad_left, grad_right, grad_mag.reshape(width))


def solution(mesh):
    fine = Mesh(mesh.devices.reshape(NY, NX, NZ, 2), ("din", "x", "z", "layer"))
    return jax.shard_map(
        local,
        mesh=fine,
        in_specs=(
            P(("layer", "x", "z"), "din"),
            P(("layer", "din"), ("x", "z")),
            P(("layer", "din"), ("x", "z")),
            P(("layer", "din"), None),
            P("layer", ("x", "z")),
            P(("layer", "x", "z")),
        ),
        out_specs=(
            P(("layer", "x", "z"), "din"),
            P(("layer", "din", "x", "z"), None),
            P(("layer", "din"), ("x", "z")),
            P(("layer", "x", "z")),
        ),
        check_vma=False,
    )
```

```python
import jax
import jax.numpy as jnp
from jax import lax
from jax.experimental import pallas as pl
from jax.experimental.pallas import tpu as pltpu
from jax.sharding import Mesh, PartitionSpec as P

F32 = jnp.float32
BF16 = jnp.bfloat16
NX, NY, NZ = 4, 8, 8
NT = (((1,), (1,)), ((), ()))
TN = (((0,), (0,)), ((), ()))
NN = (((1,), (0,)), ((), ()))
VMEM = pl.BlockSpec(memory_space=pltpu.VMEM)
SMEM = pl.BlockSpec(memory_space=pltpu.SMEM)
HBM = pl.BlockSpec(memory_space=pltpu.HBM)
MIB = 1024 * 1024
STEP = 256
HOPS = (0, 1, 3, 2)


def dot(a, b, dims):
    return lax.dot_general(a, b, dims, preferred_element_type=F32)


def shape(dims, dtype=BF16):
    return jax.ShapeDtypeStruct(dims, dtype)


def call(body, outs, flops, *args, far=(), scratch=(), out_specs=None, limit=16):
    moved = sum(a.size * a.dtype.itemsize for a in args)
    moved += sum(o.size * o.dtype.itemsize for o in outs)
    specs = [
        HBM if i in far else SMEM if a.dtype == jnp.int32 else VMEM
        for i, a in enumerate(args)
    ]
    return pl.pallas_call(
        body,
        out_shape=outs,
        in_specs=specs,
        out_specs=out_specs or [VMEM] * len(outs),
        scratch_shapes=scratch,
        compiler_params=pltpu.CompilerParams(vmem_limit_bytes=limit * MIB),
        cost_estimate=pl.CostEstimate(
            flops=flops, bytes_accessed=moved, transcendentals=0
        ),
    )(*args)


def fetch(pairs, sems):
    copies = [
        pltpu.make_async_copy(src, dst, sems.at[i]) for i, (src, dst) in enumerate(pairs)
    ]
    for copy in copies:
        copy.start()
    return copies


def two_rows(value, width):
    high = value.astype(BF16).astype(F32)
    row = lax.broadcasted_iota(jnp.int32, (16, width), 0)
    return jnp.where(row == 0, high, jnp.where(row == 1, value - high, 0.0)).astype(BF16)


def merge_body(
    w_hbm, at_hbm, b_hbm, g_hbm, acts_hbm, pay_ref, many_hbm, w_ref, at_ref, b_ref, g_ref, acts_ref, sems, more
):
    copies = fetch(
        (
            (acts_hbm, acts_ref),
            (w_hbm, w_ref),
            (at_hbm, at_ref),
            (b_hbm, b_ref),
            (g_hbm, g_ref),
        ),
        sems,
    )
    copies[0].wait()
    repeats = fetch([(acts_ref, many_hbm.at[z]) for z in range(NZ)], more)
    for copy in copies[1:]:
        copy.wait()
    din, width = w_ref.shape
    tokens = g_ref.shape[0]
    total = jnp.zeros((1, width), F32)
    for i in range(0, din, STEP):
        merged = w_ref[pl.ds(i, STEP), :].astype(F32) + dot(
            at_ref[:, pl.ds(i, STEP)], b_ref[...], TN
        )
        total += jnp.sum(merged * merged, axis=0, keepdims=True)
    tail = two_rows(total, width)
    for y in range(NY):
        pay_ref[y, pl.ds(0, tokens), :] = g_ref[...]
        pay_ref[y, pl.ds(tokens, 16), :] = tail
    for copy in repeats:
        copy.wait()


def scale_body(x_ref, got_ref, mag_ref, b_ref, *outs):
    tokens = got_ref.shape[1] - 16
    width = got_ref.shape[2]
    squares = jnp.zeros((16, width), F32)
    for y in range(NY):
        squares += got_ref[y, pl.ds(tokens, 16), :].astype(F32)
    squares = jnp.sum(squares, axis=0, keepdims=True)
    scale = mag_ref[...] / jnp.sqrt(squares)
    half = NY // NX
    for hop, out in zip(HOPS, outs):
        block = lax.rem(x_ref[0] + hop, NX)
        for h in range(half):
            out[pl.ds(h * tokens, tokens), :] = (
                got_ref[block * half + h, pl.ds(0, tokens), :].astype(F32) * scale
            ).astype(BF16)
        out[pl.ds(half * tokens, b_ref.shape[0]), :] = b_ref[...]


def source(x_ref, k):
    return lax.rem(x_ref[0] + NX - HOPS[k], NX)


def acts_body(
    x_ref, s0, s1, s2, s3, wide, at, whole, out_hbm, *rest
):
    side_hbm, (out, lefts, sides, out_sems, side_sems) = rest[:NX], rest[NX:]
    blocks = (s0, s1, s2, s3)
    tokens, din = whole.shape
    rank = at.shape[0]
    steps = din // STEP
    place = [source(x_ref, k) for k in range(NX)]
    low = jnp.zeros((tokens, NX * rank), F32)
    for s in blocks:
        b = s[pl.ds(tokens, rank), :]
        low += dot(s[pl.ds(0, tokens), :], jnp.concatenate([b] * NX, axis=0), NT)
    low = low.astype(BF16)
    sends = []

    def send(start, count):
        sends.append(
            pltpu.make_async_copy(
                out.at[:, pl.ds(start, count)],
                out_hbm.at[:, pl.ds(start, count)],
                out_sems.at[len(sends)],
            )
        )
        sends[-1].start()

    group = lax.div(lax.broadcasted_iota(jnp.int32, (8, NX * rank), 1), rank)
    each = din // NX
    rows = each // NZ
    for q in range(NX):
        left = dot(whole[:, pl.ds(q * each, each)], low, TN)
        for z in range(NZ):
            piece = jnp.zeros((8, NX * rank), F32)
            for g in range(rows // 8):
                first = z * rows + g * 8
                piece += jnp.where(group == g, left[first : first + 8], 0.0)
            lefts[pl.ds(z * rows + q * 8, 8), :] = piece
    out[:, pl.ds(din, NX * rank)] = lefts[...].astype(BF16)
    send(din, NX * rank)
    for i in range(steps):
        total = dot(low[:, :rank], at[:, pl.ds(i * STEP, STEP)], NN)
        for k, s in enumerate(blocks):
            total += dot(
                s[pl.ds(0, tokens), :], wide[place[k], pl.ds(i * STEP, STEP), :], NT
            )
        out[:, pl.ds(i * STEP, STEP)] = total.astype(BF16)
        send(i * STEP, STEP)
    down = dot(whole[...], at[...], NT).astype(BF16)
    for k, s in enumerate(blocks):
        scaled = s[pl.ds(0, tokens), :]
        outputs = dot(whole[...], wide[place[k]], NN) + dot(
            down, s[pl.ds(tokens, rank), :], NN
        )
        stat = jnp.sum(scaled.astype(F32) * outputs, axis=0, keepdims=True)
        sides[k, pl.ds(0, rank), :] = dot(down, scaled, TN).astype(BF16)
        sides[k, pl.ds(rank, 16), :] = two_rows(stat, stat.shape[1])
        sends.append(pltpu.make_async_copy(sides.at[k], side_hbm[k], side_sems.at[k]))
        sends[-1].start()
    for copy in sends:
        copy.wait()


def meet_body(r0, r1, r2, r3, pay_ref):
    rows, width = r0.shape
    total = sum(r[...].astype(F32) for r in (r0, r1, r2, r3))
    stat = jnp.sum(total[rows - 16 :], axis=0, keepdims=True)
    tail = two_rows(stat, width).astype(F32)[:8]
    each = (rows - 16) // NY
    for y in range(NY):
        pay_ref[y, :, :] = jnp.concatenate(
            [total[y * each : (y + 1) * each], tail], axis=0
        ).astype(BF16)


def sum_body(x_ref, got_ref, acts_ref, keep_ref, send_ref, lefts):
    din = acts_ref.shape[1]
    total = sum(got_ref[z].astype(F32) for z in range(NZ))
    acts_ref[...] = total[:, :din].astype(BF16)
    lefts[...] = total[:, din:]

    def block(mask):
        x = jnp.bitwise_xor(x_ref[0], mask)
        return lefts[pl.ds(pl.multiple_of(x * 8, 8), 8), :]

    keep_ref[...] = jnp.concatenate([block(0), block(3)], axis=0)
    send_ref[...] = jnp.concatenate([block(1), block(2)], axis=0).astype(BF16)


def pair_body(keep_ref, got_ref, own_ref, send_ref):
    total = keep_ref[...] + got_ref[...].astype(F32)
    own_ref[...] = total[:8]
    send_ref[...] = jnp.concatenate([total[8:], total[8:]], axis=0).astype(BF16)


def last_body(own_ref, more_ref, got_ref, mag_ref, left_ref, right_ref, mag_out):
    total = sum(got_ref[y].astype(F32) for y in range(NY))
    right_ref[...] = total[:8]
    mag_out[...] = (total[8:9] + total[9:10]) / mag_ref[...]
    left = own_ref[...] + more_ref[...].astype(F32)[:8]
    rank = left_ref.shape[1]
    for g in range(left_ref.shape[0] // 8):
        left_ref[pl.ds(g * 8, 8), :] = left[:, g * rank : (g + 1) * rank]


def shift(block, hop):
    return lax.ppermute(block, "x", [(i, (i + hop) % NX) for i in range(NX)])


def swap(block, mask):
    return lax.ppermute(block, "x", [(i, i ^ mask) for i in range(NX)])


def after(value, *others):
    return lax.optimization_barrier((value, *others))[0]


def local(acts, grad_y, w_base, a_left, b_right, magnitude):
    rows, din = acts.shape
    width = grad_y.shape[1]
    rank = a_left.shape[1]
    tokens = rows * NZ
    wider = din + NX * rank
    spot = lax.axis_index("x").astype(jnp.int32).reshape(1)
    mags = magnitude.reshape(1, width)
    a_turned = a_left.T
    wide = lax.all_gather(w_base, "x")
    parts = (w_base, a_turned, b_right, grad_y)
    pay, many = call(
        merge_body,
        [shape((NY, grad_y.shape[0] + 16, width)), shape((NZ, rows, din))],
        2 * din * width * rank,
        *parts, acts,
        far=(0, 1, 2, 3, 4),
        out_specs=[VMEM, HBM],
        scratch=[pltpu.VMEM(p.shape, p.dtype) for p in (*parts, acts)]
        + [pltpu.SemaphoreType.DMA((5,)), pltpu.SemaphoreType.DMA((NZ,))],
        limit=60,
    )
    got = lax.all_to_all(pay, "din", 0, 0, tiled=True)
    scaled = call(
        scale_body,
        [shape((tokens + rank, width))] * NX,
        4 * tokens * width * NX,
        spot, got, mags, b_right,
    )
    blocks = [scaled[0]] + [shift(scaled[k], HOPS[k]) for k in range(1, NX)]
    whole = lax.all_to_all(after(many, got), "z", 0, 0, tiled=True).reshape(tokens, din)
    part, *sides = call(
        acts_body,
        [shape((tokens, wider))] + [shape((rank + 16, width))] * NX,
        4 * tokens * din * width * NX,
        spot, *blocks, wide, a_turned, whole,
        out_specs=[HBM] * (1 + NX),
        scratch=[
            pltpu.VMEM((tokens, wider), BF16),
            pltpu.VMEM((tokens, NX * rank), F32),
            pltpu.VMEM((NX, rank + 16, width), BF16),
            pltpu.SemaphoreType.DMA((1 + din // STEP,)),
            pltpu.SemaphoreType.DMA((NX,)),
        ],
        limit=16,
    )
    back = lax.all_to_all(part.reshape(NZ, rows, wider), "z", 0, 0, tiled=True)
    met = [sides[0]] + [shift(sides[k], NX - HOPS[k]) for k in range(1, NX)]
    summed, keep, send = call(
        sum_body,
        [shape((rows, din)), shape((16, width), F32), shape((16, width))],
        0,
        spot, back,
        scratch=[pltpu.VMEM((rows, NX * rank), F32)],
    )
    more = swap(send, 1)
    (pay,) = call(meet_body, [shape((NY, 16, width))], 0, *met)
    right = lax.all_to_all(after(pay, send), "din", 0, 0, tiled=True)
    own, send = call(
        pair_body, [shape((8, width), F32), shape((16, width))], 0, keep, more
    )
    grad_left, grad_right, grad_mag = call(
        last_body,
        [shape((rows, rank), F32), shape((rank // NY, width), F32), shape((1, width), F32)],
        0,
        own, swap(send, 3), right, mags,
    )
    return (summed, grad_left, grad_right, grad_mag.reshape(width))


def solution(mesh):
    fine = Mesh(mesh.devices.reshape(NY, NX, NZ, 2), ("din", "x", "z", "layer"))
    return jax.shard_map(
        local,
        mesh=fine,
        in_specs=(
            P(("layer", "x", "z"), "din"),
            P(("layer", "din"), ("x", "z")),
            P(("layer", "din"), ("x", "z")),
            P(("layer", "din"), None),
            P("layer", ("x", "z")),
            P(("layer", "x", "z")),
        ),
        out_specs=(
            P(("layer", "x", "z"), "din"),
            P(("layer", "din", "x", "z"), None),
            P(("layer", "din"), ("x", "z")),
            P(("layer", "x", "z")),
        ),
        check_vma=False,
    )
```

```python
import jax
import jax.numpy as jnp
from jax import lax
from jax.experimental import pallas as pl
from jax.experimental.pallas import tpu as pltpu
from jax.sharding import Mesh, PartitionSpec as P

F32 = jnp.float32
BF16 = jnp.bfloat16
NX, NY, NZ = 4, 8, 8
NT = (((1,), (1,)), ((), ()))
TN = (((0,), (0,)), ((), ()))
NN = (((1,), (0,)), ((), ()))
VMEM = pl.BlockSpec(memory_space=pltpu.VMEM)
SMEM = pl.BlockSpec(memory_space=pltpu.SMEM)
HBM = pl.BlockSpec(memory_space=pltpu.HBM)
MIB = 1024 * 1024
STEP = 256
HOPS = (0, 1, 3, 2)


def dot(a, b, dims):
    return lax.dot_general(a, b, dims, preferred_element_type=F32)


def shape(dims, dtype=BF16):
    return jax.ShapeDtypeStruct(dims, dtype)


def call(body, outs, flops, *args, far=(), scratch=(), out_specs=None, limit=16):
    moved = sum(a.size * a.dtype.itemsize for a in args)
    moved += sum(o.size * o.dtype.itemsize for o in outs)
    specs = [
        HBM if i in far else SMEM if a.dtype == jnp.int32 else VMEM
        for i, a in enumerate(args)
    ]
    return pl.pallas_call(
        body,
        out_shape=outs,
        in_specs=specs,
        out_specs=out_specs or [VMEM] * len(outs),
        scratch_shapes=scratch,
        compiler_params=pltpu.CompilerParams(vmem_limit_bytes=limit * MIB),
        cost_estimate=pl.CostEstimate(
            flops=flops, bytes_accessed=moved, transcendentals=0
        ),
    )(*args)


def fetch(pairs, sems):
    copies = [
        pltpu.make_async_copy(src, dst, sems.at[i]) for i, (src, dst) in enumerate(pairs)
    ]
    for copy in copies:
        copy.start()
    return copies


def two_rows(value, width):
    high = value.astype(BF16).astype(F32)
    row = lax.broadcasted_iota(jnp.int32, (16, width), 0)
    return jnp.where(row == 0, high, jnp.where(row == 1, value - high, 0.0)).astype(BF16)


def merge_body(
    w_hbm, at_hbm, b_hbm, g_hbm, acts_hbm, pay_ref, many_hbm, w_ref, at_ref, b_ref, g_ref, acts_ref, sems, more
):
    copies = fetch(
        (
            (acts_hbm, acts_ref),
            (w_hbm, w_ref),
            (at_hbm, at_ref),
            (b_hbm, b_ref),
            (g_hbm, g_ref),
        ),
        sems,
    )
    copies[0].wait()
    repeats = fetch([(acts_ref, many_hbm.at[z]) for z in range(NZ)], more)
    for copy in copies[1:]:
        copy.wait()
    din, width = w_ref.shape
    tokens = g_ref.shape[0]
    total = jnp.zeros((1, width), F32)
    for i in range(0, din, STEP):
        merged = w_ref[pl.ds(i, STEP), :].astype(F32) + dot(
            at_ref[:, pl.ds(i, STEP)], b_ref[...], TN
        )
        total += jnp.sum(merged * merged, axis=0, keepdims=True)
    tail = two_rows(total, width)
    for y in range(NY):
        pay_ref[y, pl.ds(0, tokens), :] = g_ref[...]
        pay_ref[y, pl.ds(tokens, 16), :] = tail
    for copy in repeats:
        copy.wait()


def scale_body(x_ref, got_ref, mag_ref, b_ref, *outs):
    tokens = got_ref.shape[1] - 16
    width = got_ref.shape[2]
    squares = jnp.zeros((16, width), F32)
    for y in range(NY):
        squares += got_ref[y, pl.ds(tokens, 16), :].astype(F32)
    squares = jnp.sum(squares, axis=0, keepdims=True)
    scale = mag_ref[...] / jnp.sqrt(squares)
    half = NY // NX
    for hop, out in zip(HOPS, outs):
        block = lax.rem(x_ref[0] + hop, NX)
        for h in range(half):
            out[pl.ds(h * tokens, tokens), :] = (
                got_ref[block * half + h, pl.ds(0, tokens), :].astype(F32) * scale
            ).astype(BF16)
        out[pl.ds(half * tokens, b_ref.shape[0]), :] = b_ref[...]


def bring_body(wide_hbm, out_ref, sems):
    for copy in fetch([(wide_hbm.at[k], out_ref.at[k]) for k in range(NX)], sems):
        copy.wait()


def source(x_ref, k):
    return lax.rem(x_ref[0] + NX - HOPS[k], NX)


def acts_body(
    x_ref, s0, s1, s2, s3, wide, at, whole, out_hbm, *rest
):
    side_hbm, (out, lefts, sides, out_sems, side_sems) = rest[:NX], rest[NX:]
    blocks = (s0, s1, s2, s3)
    tokens, din = whole.shape
    rank = at.shape[0]
    steps = din // STEP
    place = [source(x_ref, k) for k in range(NX)]
    low = jnp.zeros((tokens, NX * rank), F32)
    for s in blocks:
        b = s[pl.ds(tokens, rank), :]
        low += dot(s[pl.ds(0, tokens), :], jnp.concatenate([b] * NX, axis=0), NT)
    low = low.astype(BF16)
    sends = []

    def send(start, count):
        sends.append(
            pltpu.make_async_copy(
                out.at[:, pl.ds(start, count)],
                out_hbm.at[:, pl.ds(start, count)],
                out_sems.at[len(sends)],
            )
        )
        sends[-1].start()

    group = lax.div(lax.broadcasted_iota(jnp.int32, (8, NX * rank), 1), rank)
    each = din // NX
    rows = each // NZ
    for q in range(NX):
        left = dot(whole[:, pl.ds(q * each, each)], low, TN)
        for z in range(NZ):
            piece = jnp.zeros((8, NX * rank), F32)
            for g in range(rows // 8):
                first = z * rows + g * 8
                piece += jnp.where(group == g, left[first : first + 8], 0.0)
            lefts[pl.ds(z * rows + q * 8, 8), :] = piece
    out[:, pl.ds(din, NX * rank)] = lefts[...].astype(BF16)
    send(din, NX * rank)
    for i in range(steps):
        total = dot(low[:, :rank], at[:, pl.ds(i * STEP, STEP)], NN)
        for k, s in enumerate(blocks):
            total += dot(
                s[pl.ds(0, tokens), :], wide[place[k], pl.ds(i * STEP, STEP), :], NT
            )
        out[:, pl.ds(i * STEP, STEP)] = total.astype(BF16)
        send(i * STEP, STEP)
    down = dot(whole[...], at[...], NT).astype(BF16)
    for k, s in enumerate(blocks):
        scaled = s[pl.ds(0, tokens), :]
        outputs = dot(whole[...], wide[place[k]], NN) + dot(
            down, s[pl.ds(tokens, rank), :], NN
        )
        stat = jnp.sum(scaled.astype(F32) * outputs, axis=0, keepdims=True)
        sides[k, pl.ds(0, rank), :] = dot(down, scaled, TN).astype(BF16)
        sides[k, pl.ds(rank, 16), :] = two_rows(stat, stat.shape[1])
        sends.append(pltpu.make_async_copy(sides.at[k], side_hbm[k], side_sems.at[k]))
        sends[-1].start()
    for copy in sends:
        copy.wait()


def meet_body(r0, r1, r2, r3, pay_ref):
    rows, width = r0.shape
    total = sum(r[...].astype(F32) for r in (r0, r1, r2, r3))
    stat = jnp.sum(total[rows - 16 :], axis=0, keepdims=True)
    tail = two_rows(stat, width).astype(F32)[:8]
    each = (rows - 16) // NY
    for y in range(NY):
        pay_ref[y, :, :] = jnp.concatenate(
            [total[y * each : (y + 1) * each], tail], axis=0
        ).astype(BF16)


def sum_body(x_ref, got_ref, acts_ref, keep_ref, send_ref, lefts):
    din = acts_ref.shape[1]
    total = sum(got_ref[z].astype(F32) for z in range(NZ))
    acts_ref[...] = total[:, :din].astype(BF16)
    lefts[...] = total[:, din:]

    def block(mask):
        x = jnp.bitwise_xor(x_ref[0], mask)
        return lefts[pl.ds(pl.multiple_of(x * 8, 8), 8), :]

    keep_ref[...] = jnp.concatenate([block(0), block(3)], axis=0)
    send_ref[...] = jnp.concatenate([block(1), block(2)], axis=0).astype(BF16)


def pair_body(keep_ref, got_ref, own_ref, send_ref):
    total = keep_ref[...] + got_ref[...].astype(F32)
    own_ref[...] = total[:8]
    send_ref[...] = jnp.concatenate([total[8:], total[8:]], axis=0).astype(BF16)


def last_body(own_ref, more_ref, got_ref, mag_ref, left_ref, right_ref, mag_out):
    total = sum(got_ref[y].astype(F32) for y in range(NY))
    right_ref[...] = total[:8]
    mag_out[...] = (total[8:9] + total[9:10]) / mag_ref[...]
    left = own_ref[...] + more_ref[...].astype(F32)[:8]
    rank = left_ref.shape[1]
    for g in range(left_ref.shape[0] // 8):
        left_ref[pl.ds(g * 8, 8), :] = left[:, g * rank : (g + 1) * rank]


def shift(block, hop):
    return lax.ppermute(block, "x", [(i, (i + hop) % NX) for i in range(NX)])


def swap(block, mask):
    return lax.ppermute(block, "x", [(i, i ^ mask) for i in range(NX)])


def after(value, *others):
    return lax.optimization_barrier((value, *others))[0]


def local(acts, grad_y, w_base, a_left, b_right, magnitude):
    rows, din = acts.shape
    width = grad_y.shape[1]
    rank = a_left.shape[1]
    tokens = rows * NZ
    wider = din + NX * rank
    spot = lax.axis_index("x").astype(jnp.int32).reshape(1)
    mags = magnitude.reshape(1, width)
    a_turned = a_left.T
    wide = lax.all_gather(w_base, "x")
    parts = (w_base, a_turned, b_right, grad_y)
    pay, many = call(
        merge_body,
        [shape((NY, grad_y.shape[0] + 16, width)), shape((NZ, rows, din))],
        2 * din * width * rank,
        *parts, acts,
        far=(0, 1, 2, 3, 4),
        out_specs=[VMEM, HBM],
        scratch=[pltpu.VMEM(p.shape, p.dtype) for p in (*parts, acts)]
        + [pltpu.SemaphoreType.DMA((5,)), pltpu.SemaphoreType.DMA((NZ,))],
        limit=60,
    )
    got = lax.all_to_all(pay, "din", 0, 0, tiled=True)
    scaled = call(
        scale_body,
        [shape((tokens + rank, width))] * NX,
        4 * tokens * width * NX,
        spot, got, mags, b_right,
    )
    blocks = [scaled[0]] + [shift(scaled[k], HOPS[k]) for k in range(1, NX)]
    whole = lax.all_to_all(after(many, got), "z", 0, 0, tiled=True).reshape(tokens, din)
    (wide,) = call(
        bring_body,
        [shape(wide.shape)],
        0,
        wide,
        far=(0,),
        scratch=[pltpu.SemaphoreType.DMA((NX,))],
        limit=4,
    )
    part, *sides = call(
        acts_body,
        [shape((tokens, wider))] + [shape((rank + 16, width))] * NX,
        4 * tokens * din * width * NX,
        spot, *blocks, wide, a_turned, whole,
        out_specs=[HBM] * (1 + NX),
        scratch=[
            pltpu.VMEM((tokens, wider), BF16),
            pltpu.VMEM((tokens, NX * rank), F32),
            pltpu.VMEM((NX, rank + 16, width), BF16),
            pltpu.SemaphoreType.DMA((1 + din // STEP,)),
            pltpu.SemaphoreType.DMA((NX,)),
        ],
        limit=16,
    )
    back = lax.all_to_all(part.reshape(NZ, rows, wider), "z", 0, 0, tiled=True)
    met = [sides[0]] + [shift(sides[k], NX - HOPS[k]) for k in range(1, NX)]
    summed, keep, send = call(
        sum_body,
        [shape((rows, din)), shape((16, width), F32), shape((16, width))],
        0,
        spot, back,
        scratch=[pltpu.VMEM((rows, NX * rank), F32)],
    )
    more = swap(send, 1)
    (pay,) = call(meet_body, [shape((NY, 16, width))], 0, *met)
    right = lax.all_to_all(after(pay, send), "din", 0, 0, tiled=True)
    own, send = call(
        pair_body, [shape((8, width), F32), shape((16, width))], 0, keep, more
    )
    grad_left, grad_right, grad_mag = call(
        last_body,
        [shape((rows, rank), F32), shape((rank // NY, width), F32), shape((1, width), F32)],
        0,
        own, swap(send, 3), right, mags,
    )
    return (summed, grad_left, grad_right, grad_mag.reshape(width))


def solution(mesh):
    fine = Mesh(mesh.devices.reshape(NY, NX, NZ, 2), ("din", "x", "z", "layer"))
    return jax.shard_map(
        local,
        mesh=fine,
        in_specs=(
            P(("layer", "x", "z"), "din"),
            P(("layer", "din"), ("x", "z")),
            P(("layer", "din"), ("x", "z")),
            P(("layer", "din"), None),
            P("layer", ("x", "z")),
            P(("layer", "x", "z")),
        ),
        out_specs=(
            P(("layer", "x", "z"), "din"),
            P(("layer", "din", "x", "z"), None),
            P(("layer", "din"), ("x", "z")),
            P(("layer", "x", "z")),
        ),
        check_vma=False,
    )
```

```python
import jax
import jax.numpy as jnp
from jax import lax
from jax.experimental import pallas as pl
from jax.experimental.pallas import tpu as pltpu
from jax.sharding import Mesh, PartitionSpec as P

F32 = jnp.float32
BF16 = jnp.bfloat16
NX, NY, NZ = 4, 8, 8
NT = (((1,), (1,)), ((), ()))
TN = (((0,), (0,)), ((), ()))
NN = (((1,), (0,)), ((), ()))
VMEM = pl.BlockSpec(memory_space=pltpu.VMEM)
SMEM = pl.BlockSpec(memory_space=pltpu.SMEM)
HBM = pl.BlockSpec(memory_space=pltpu.HBM)
MIB = 1024 * 1024
STEP = 256
HOPS = (0, 1, 3, 2)


def dot(a, b, dims):
    return lax.dot_general(a, b, dims, preferred_element_type=F32)


def shape(dims, dtype=BF16):
    return jax.ShapeDtypeStruct(dims, dtype)


def call(body, outs, flops, *args, far=(), scratch=(), out_specs=None, limit=16):
    moved = sum(a.size * a.dtype.itemsize for a in args)
    moved += sum(o.size * o.dtype.itemsize for o in outs)
    specs = [
        HBM if i in far else SMEM if a.dtype == jnp.int32 else VMEM
        for i, a in enumerate(args)
    ]
    return pl.pallas_call(
        body,
        out_shape=outs,
        in_specs=specs,
        out_specs=out_specs or [VMEM] * len(outs),
        scratch_shapes=scratch,
        compiler_params=pltpu.CompilerParams(vmem_limit_bytes=limit * MIB),
        cost_estimate=pl.CostEstimate(
            flops=flops, bytes_accessed=moved, transcendentals=0
        ),
    )(*args)


def fetch(pairs, sems):
    copies = [
        pltpu.make_async_copy(src, dst, sems.at[i]) for i, (src, dst) in enumerate(pairs)
    ]
    for copy in copies:
        copy.start()
    return copies


def two_rows(value, width):
    high = value.astype(BF16).astype(F32)
    row = lax.broadcasted_iota(jnp.int32, (16, width), 0)
    return jnp.where(row == 0, high, jnp.where(row == 1, value - high, 0.0)).astype(BF16)


def merge_body(
    w_hbm, at_hbm, b_hbm, g_hbm, acts_hbm, pay_ref, many_hbm, w_ref, at_ref, b_ref, g_ref, acts_ref, sems, more
):
    copies = fetch(
        (
            (acts_hbm, acts_ref),
            (w_hbm, w_ref),
            (at_hbm, at_ref),
            (b_hbm, b_ref),
            (g_hbm, g_ref),
        ),
        sems,
    )
    copies[0].wait()
    repeats = fetch([(acts_ref, many_hbm.at[z]) for z in range(NZ)], more)
    for copy in copies[1:]:
        copy.wait()
    din, width = w_ref.shape
    tokens = g_ref.shape[0]
    total = jnp.zeros((1, width), F32)
    for i in range(0, din, STEP):
        merged = w_ref[pl.ds(i, STEP), :].astype(F32) + dot(
            at_ref[:, pl.ds(i, STEP)], b_ref[...], TN
        )
        total += jnp.sum(merged * merged, axis=0, keepdims=True)
    tail = two_rows(total, width)
    for y in range(NY):
        pay_ref[y, pl.ds(0, tokens), :] = g_ref[...]
        pay_ref[y, pl.ds(tokens, 16), :] = tail
    for copy in repeats:
        copy.wait()


def scale_body(x_ref, got_ref, mag_ref, b_ref, *outs):
    tokens = got_ref.shape[1] - 16
    width = got_ref.shape[2]
    squares = jnp.zeros((16, width), F32)
    for y in range(NY):
        squares += got_ref[y, pl.ds(tokens, 16), :].astype(F32)
    squares = jnp.sum(squares, axis=0, keepdims=True)
    scale = mag_ref[...] / jnp.sqrt(squares)
    half = NY // NX
    for hop, out in zip(HOPS, outs):
        block = lax.rem(x_ref[0] + hop, NX)
        for h in range(half):
            out[pl.ds(h * tokens, tokens), :] = (
                got_ref[block * half + h, pl.ds(0, tokens), :].astype(F32) * scale
            ).astype(BF16)
        out[pl.ds(half * tokens, b_ref.shape[0]), :] = b_ref[...]


def bring_body(wide_hbm, out_ref, sems):
    for copy in fetch([(wide_hbm.at[k], out_ref.at[k]) for k in range(NX)], sems):
        copy.wait()


def source(x_ref, k):
    return lax.rem(x_ref[0] + NX - HOPS[k], NX)


def acts_body(
    x_ref, s0, s1, s2, s3, wide, at, whole, out_hbm, *rest
):
    side_hbm, (out, lefts, sides, out_sems, side_sems) = rest[:NX], rest[NX:]
    blocks = (s0, s1, s2, s3)
    tokens, din = whole.shape
    rank = at.shape[0]
    steps = din // STEP
    place = [source(x_ref, k) for k in range(NX)]
    low = jnp.zeros((tokens, NX * rank), F32)
    for s in blocks:
        b = s[pl.ds(tokens, rank), :]
        low += dot(s[pl.ds(0, tokens), :], jnp.concatenate([b] * NX, axis=0), NT)
    low = low.astype(BF16)
    sends = []

    def send(start, count):
        sends.append(
            pltpu.make_async_copy(
                out.at[:, pl.ds(start, count)],
                out_hbm.at[:, pl.ds(start, count)],
                out_sems.at[len(sends)],
            )
        )
        sends[-1].start()

    group = lax.div(lax.broadcasted_iota(jnp.int32, (8, NX * rank), 1), rank)
    each = din // NX
    rows = each // NZ
    for q in range(NX):
        left = dot(whole[:, pl.ds(q * each, each)], low, TN)
        for z in range(NZ):
            piece = jnp.zeros((8, NX * rank), F32)
            for g in range(rows // 8):
                first = z * rows + g * 8
                piece += jnp.where(group == g, left[first : first + 8], 0.0)
            lefts[pl.ds(z * rows + q * 8, 8), :] = piece
    out[:, pl.ds(din, NX * rank)] = lefts[...].astype(BF16)
    send(din, NX * rank)
    for i in range(steps):
        total = dot(low[:, :rank], at[:, pl.ds(i * STEP, STEP)], NN)
        for k, s in enumerate(blocks):
            total += dot(
                s[pl.ds(0, tokens), :], wide[place[k], pl.ds(i * STEP, STEP), :], NT
            )
        out[:, pl.ds(i * STEP, STEP)] = total.astype(BF16)
        send(i * STEP, STEP)
    down = dot(whole[...], at[...], NT).astype(BF16)
    for k, s in enumerate(blocks):
        scaled = s[pl.ds(0, tokens), :]
        outputs = dot(whole[...], wide[place[k]], NN) + dot(
            down, s[pl.ds(tokens, rank), :], NN
        )
        stat = jnp.sum(scaled.astype(F32) * outputs, axis=0, keepdims=True)
        sides[k, pl.ds(0, rank), :] = dot(down, scaled, TN).astype(BF16)
        sides[k, pl.ds(rank, 16), :] = two_rows(stat, stat.shape[1])
        sends.append(pltpu.make_async_copy(sides.at[k], side_hbm[k], side_sems.at[k]))
        sends[-1].start()
    for copy in sends:
        copy.wait()


def meet_body(r0, r1, r2, r3, pay_ref):
    rows, width = r0.shape
    total = sum(r[...].astype(F32) for r in (r0, r1, r2, r3))
    stat = jnp.sum(total[rows - 16 :], axis=0, keepdims=True)
    tail = two_rows(stat, width).astype(F32)[:8]
    each = (rows - 16) // NY
    for y in range(NY):
        pay_ref[y, :, :] = jnp.concatenate(
            [total[y * each : (y + 1) * each], tail], axis=0
        ).astype(BF16)


def sum_body(x_ref, got_ref, acts_ref, keep_ref, send_ref, lefts):
    din = acts_ref.shape[1]
    total = sum(got_ref[z].astype(F32) for z in range(NZ))
    acts_ref[...] = total[:, :din].astype(BF16)
    lefts[...] = total[:, din:]

    def block(mask):
        x = jnp.bitwise_xor(x_ref[0], mask)
        return lefts[pl.ds(pl.multiple_of(x * 8, 8), 8), :]

    keep_ref[...] = jnp.concatenate([block(0), block(3)], axis=0)
    send_ref[...] = jnp.concatenate([block(1), block(2)], axis=0).astype(BF16)


def pair_body(keep_ref, got_ref, own_ref, send_ref):
    total = keep_ref[...] + got_ref[...].astype(F32)
    own_ref[...] = total[:8]
    send_ref[...] = jnp.concatenate([total[8:], total[8:]], axis=0).astype(BF16)


def last_body(own_ref, more_ref, got_ref, mag_ref, left_ref, right_ref, mag_out):
    total = sum(got_ref[y].astype(F32) for y in range(NY))
    right_ref[...] = total[:8]
    mag_out[...] = (total[8:9] + total[9:10]) / mag_ref[...]
    left = own_ref[...] + more_ref[...].astype(F32)[:8]
    rank = left_ref.shape[1]
    for g in range(left_ref.shape[0] // 8):
        left_ref[pl.ds(g * 8, 8), :] = left[:, g * rank : (g + 1) * rank]


def shift(block, hop):
    return lax.ppermute(block, "x", [(i, (i + hop) % NX) for i in range(NX)])


def swap(block, mask):
    return lax.ppermute(block, "x", [(i, i ^ mask) for i in range(NX)])


def after(value, *others):
    return lax.optimization_barrier((value, *others))[0]


def local(acts, grad_y, w_base, a_left, b_right, magnitude):
    rows, din = acts.shape
    width = grad_y.shape[1]
    rank = a_left.shape[1]
    tokens = rows * NZ
    wider = din + NX * rank
    spot = lax.axis_index("x").astype(jnp.int32).reshape(1)
    mags = magnitude.reshape(1, width)
    a_turned = a_left.T
    wide = lax.all_gather(w_base, "x")
    parts = (w_base, a_turned, b_right, grad_y)
    pay, many = call(
        merge_body,
        [shape((NY, grad_y.shape[0] + 16, width)), shape((NZ, rows, din))],
        2 * din * width * rank,
        *parts, acts,
        far=(0, 1, 2, 3, 4),
        out_specs=[VMEM, HBM],
        scratch=[pltpu.VMEM(p.shape, p.dtype) for p in (*parts, acts)]
        + [pltpu.SemaphoreType.DMA((5,)), pltpu.SemaphoreType.DMA((NZ,))],
        limit=60,
    )
    got = lax.all_to_all(pay, "din", 0, 0, tiled=True)
    scaled = call(
        scale_body,
        [shape((tokens + rank, width))] * NX,
        4 * tokens * width * NX,
        spot, got, mags, b_right,
    )
    blocks = [scaled[0]] + [shift(scaled[k], HOPS[k]) for k in range(1, NX)]
    whole = lax.all_to_all(after(many, got), "z", 0, 0, tiled=True).reshape(tokens, din)
    (wide,) = call(
        bring_body,
        [shape(wide.shape)],
        0,
        after(wide, blocks[1]),
        far=(0,),
        scratch=[pltpu.SemaphoreType.DMA((NX,))],
        limit=4,
    )
    part, *sides = call(
        acts_body,
        [shape((tokens, wider))] + [shape((rank + 16, width))] * NX,
        4 * tokens * din * width * NX,
        spot, *blocks, wide, a_turned, whole,
        out_specs=[HBM] * (1 + NX),
        scratch=[
            pltpu.VMEM((tokens, wider), BF16),
            pltpu.VMEM((tokens, NX * rank), F32),
            pltpu.VMEM((NX, rank + 16, width), BF16),
            pltpu.SemaphoreType.DMA((1 + din // STEP,)),
            pltpu.SemaphoreType.DMA((NX,)),
        ],
        limit=16,
    )
    back = lax.all_to_all(part.reshape(NZ, rows, wider), "z", 0, 0, tiled=True)
    met = [sides[0]] + [shift(sides[k], NX - HOPS[k]) for k in range(1, NX)]
    summed, keep, send = call(
        sum_body,
        [shape((rows, din)), shape((16, width), F32), shape((16, width))],
        0,
        spot, back,
        scratch=[pltpu.VMEM((rows, NX * rank), F32)],
    )
    more = swap(send, 1)
    (pay,) = call(meet_body, [shape((NY, 16, width))], 0, *met)
    right = lax.all_to_all(after(pay, send), "din", 0, 0, tiled=True)
    own, send = call(
        pair_body, [shape((8, width), F32), shape((16, width))], 0, keep, more
    )
    grad_left, grad_right, grad_mag = call(
        last_body,
        [shape((rows, rank), F32), shape((rank // NY, width), F32), shape((1, width), F32)],
        0,
        own, swap(send, 3), right, mags,
    )
    return (summed, grad_left, grad_right, grad_mag.reshape(width))


def solution(mesh):
    fine = Mesh(mesh.devices.reshape(NY, NX, NZ, 2), ("din", "x", "z", "layer"))
    return jax.shard_map(
        local,
        mesh=fine,
        in_specs=(
            P(("layer", "x", "z"), "din"),
            P(("layer", "din"), ("x", "z")),
            P(("layer", "din"), ("x", "z")),
            P(("layer", "din"), None),
            P("layer", ("x", "z")),
            P(("layer", "x", "z")),
        ),
        out_specs=(
            P(("layer", "x", "z"), "din"),
            P(("layer", "din", "x", "z"), None),
            P(("layer", "din"), ("x", "z")),
            P(("layer", "x", "z")),
        ),
        check_vma=False,
    )
```

```python
import jax
import jax.numpy as jnp
from jax import lax
from jax.experimental import pallas as pl
from jax.experimental.pallas import tpu as pltpu
from jax.sharding import Mesh, PartitionSpec as P

F32 = jnp.float32
BF16 = jnp.bfloat16
NX, NY, NZ = 4, 8, 8
NT = (((1,), (1,)), ((), ()))
TN = (((0,), (0,)), ((), ()))
NN = (((1,), (0,)), ((), ()))
VMEM = pl.BlockSpec(memory_space=pltpu.VMEM)
SMEM = pl.BlockSpec(memory_space=pltpu.SMEM)
HBM = pl.BlockSpec(memory_space=pltpu.HBM)
MIB = 1024 * 1024
STEP = 256
HOPS = (0, 1, 3, 2)


def dot(a, b, dims):
    return lax.dot_general(a, b, dims, preferred_element_type=F32)


def shape(dims, dtype=BF16):
    return jax.ShapeDtypeStruct(dims, dtype)


def call(body, outs, flops, *args, far=(), scratch=(), out_specs=None, limit=16):
    moved = sum(a.size * a.dtype.itemsize for a in args)
    moved += sum(o.size * o.dtype.itemsize for o in outs)
    specs = [
        HBM if i in far else SMEM if a.dtype == jnp.int32 else VMEM
        for i, a in enumerate(args)
    ]
    return pl.pallas_call(
        body,
        out_shape=outs,
        in_specs=specs,
        out_specs=out_specs or [VMEM] * len(outs),
        scratch_shapes=scratch,
        compiler_params=pltpu.CompilerParams(vmem_limit_bytes=limit * MIB),
        cost_estimate=pl.CostEstimate(
            flops=flops, bytes_accessed=moved, transcendentals=0
        ),
    )(*args)


def fetch(pairs, sems):
    copies = [
        pltpu.make_async_copy(src, dst, sems.at[i]) for i, (src, dst) in enumerate(pairs)
    ]
    for copy in copies:
        copy.start()
    return copies


def two_rows(value, width):
    high = value.astype(BF16).astype(F32)
    row = lax.broadcasted_iota(jnp.int32, (16, width), 0)
    return jnp.where(row == 0, high, jnp.where(row == 1, value - high, 0.0)).astype(BF16)


def merge_body(
    w_hbm, at_hbm, b_hbm, g_hbm, pay_ref, w_ref, at_ref, b_ref, g_ref, sems
):
    copies = fetch(
        (
            (w_hbm, w_ref),
            (at_hbm, at_ref),
            (b_hbm, b_ref),
            (g_hbm, g_ref),
        ),
        sems,
    )
    for copy in copies:
        copy.wait()
    din, width = w_ref.shape
    tokens = g_ref.shape[0]
    total = jnp.zeros((1, width), F32)
    for i in range(0, din, STEP):
        merged = w_ref[pl.ds(i, STEP), :].astype(F32) + dot(
            at_ref[:, pl.ds(i, STEP)], b_ref[...], TN
        )
        total += jnp.sum(merged * merged, axis=0, keepdims=True)
    tail = two_rows(total, width)
    for y in range(NY):
        pay_ref[y, pl.ds(0, tokens), :] = g_ref[...]
        pay_ref[y, pl.ds(tokens, 16), :] = tail


def scale_body(x_ref, got_ref, mag_ref, b_ref, *outs):
    tokens = got_ref.shape[1] - 16
    width = got_ref.shape[2]
    squares = jnp.zeros((16, width), F32)
    for y in range(NY):
        squares += got_ref[y, pl.ds(tokens, 16), :].astype(F32)
    squares = jnp.sum(squares, axis=0, keepdims=True)
    scale = mag_ref[...] / jnp.sqrt(squares)
    half = NY // NX
    for hop, out in zip(HOPS, outs):
        block = lax.rem(x_ref[0] + hop, NX)
        for h in range(half):
            out[pl.ds(h * tokens, tokens), :] = (
                got_ref[block * half + h, pl.ds(0, tokens), :].astype(F32) * scale
            ).astype(BF16)
        out[pl.ds(half * tokens, b_ref.shape[0]), :] = b_ref[...]


def many_body(acts_ref, many_hbm, sems):
    for copy in fetch([(acts_ref, many_hbm.at[z]) for z in range(NZ)], sems):
        copy.wait()


def bring_body(wide_hbm, out_ref, sems):
    for copy in fetch([(wide_hbm.at[k], out_ref.at[k]) for k in range(NX)], sems):
        copy.wait()


def source(x_ref, k):
    return lax.rem(x_ref[0] + NX - HOPS[k], NX)


def acts_body(
    x_ref, s0, s1, s2, s3, wide, at, whole, out_hbm, *rest
):
    side_hbm, (out, lefts, sides, out_sems, side_sems) = rest[:NX], rest[NX:]
    blocks = (s0, s1, s2, s3)
    tokens, din = whole.shape
    rank = at.shape[0]
    steps = din // STEP
    place = [source(x_ref, k) for k in range(NX)]
    low = jnp.zeros((tokens, NX * rank), F32)
    for s in blocks:
        b = s[pl.ds(tokens, rank), :]
        low += dot(s[pl.ds(0, tokens), :], jnp.concatenate([b] * NX, axis=0), NT)
    low = low.astype(BF16)
    sends = []

    def send(start, count):
        sends.append(
            pltpu.make_async_copy(
                out.at[:, pl.ds(start, count)],
                out_hbm.at[:, pl.ds(start, count)],
                out_sems.at[len(sends)],
            )
        )
        sends[-1].start()

    group = lax.div(lax.broadcasted_iota(jnp.int32, (8, NX * rank), 1), rank)
    each = din // NX
    rows = each // NZ
    for q in range(NX):
        left = dot(whole[:, pl.ds(q * each, each)], low, TN)
        for z in range(NZ):
            piece = jnp.zeros((8, NX * rank), F32)
            for g in range(rows // 8):
                first = z * rows + g * 8
                piece += jnp.where(group == g, left[first : first + 8], 0.0)
            lefts[pl.ds(z * rows + q * 8, 8), :] = piece
    out[:, pl.ds(din, NX * rank)] = lefts[...].astype(BF16)
    send(din, NX * rank)
    for i in range(steps):
        total = dot(low[:, :rank], at[:, pl.ds(i * STEP, STEP)], NN)
        for k, s in enumerate(blocks):
            total += dot(
                s[pl.ds(0, tokens), :], wide[place[k], pl.ds(i * STEP, STEP), :], NT
            )
        out[:, pl.ds(i * STEP, STEP)] = total.astype(BF16)
        send(i * STEP, STEP)
    down = dot(whole[...], at[...], NT).astype(BF16)
    for k, s in enumerate(blocks):
        scaled = s[pl.ds(0, tokens), :]
        outputs = dot(whole[...], wide[place[k]], NN) + dot(
            down, s[pl.ds(tokens, rank), :], NN
        )
        stat = jnp.sum(scaled.astype(F32) * outputs, axis=0, keepdims=True)
        sides[k, pl.ds(0, rank), :] = dot(down, scaled, TN).astype(BF16)
        sides[k, pl.ds(rank, 16), :] = two_rows(stat, stat.shape[1])
        sends.append(pltpu.make_async_copy(sides.at[k], side_hbm[k], side_sems.at[k]))
        sends[-1].start()
    for copy in sends:
        copy.wait()


def meet_body(r0, r1, r2, r3, pay_ref):
    rows, width = r0.shape
    total = sum(r[...].astype(F32) for r in (r0, r1, r2, r3))
    stat = jnp.sum(total[rows - 16 :], axis=0, keepdims=True)
    tail = two_rows(stat, width).astype(F32)[:8]
    each = (rows - 16) // NY
    for y in range(NY):
        pay_ref[y, :, :] = jnp.concatenate(
            [total[y * each : (y + 1) * each], tail], axis=0
        ).astype(BF16)


def sum_body(x_ref, got_ref, acts_ref, keep_ref, send_ref, lefts):
    din = acts_ref.shape[1]
    total = sum(got_ref[z].astype(F32) for z in range(NZ))
    acts_ref[...] = total[:, :din].astype(BF16)
    lefts[...] = total[:, din:]

    def block(mask):
        x = jnp.bitwise_xor(x_ref[0], mask)
        return lefts[pl.ds(pl.multiple_of(x * 8, 8), 8), :]

    keep_ref[...] = jnp.concatenate([block(0), block(3)], axis=0)
    send_ref[...] = jnp.concatenate([block(1), block(2)], axis=0).astype(BF16)


def pair_body(keep_ref, got_ref, own_ref, send_ref):
    total = keep_ref[...] + got_ref[...].astype(F32)
    own_ref[...] = total[:8]
    send_ref[...] = jnp.concatenate([total[8:], total[8:]], axis=0).astype(BF16)


def last_body(own_ref, more_ref, got_ref, mag_ref, left_ref, right_ref, mag_out):
    total = sum(got_ref[y].astype(F32) for y in range(NY))
    right_ref[...] = total[:8]
    mag_out[...] = (total[8:9] + total[9:10]) / mag_ref[...]
    left = own_ref[...] + more_ref[...].astype(F32)[:8]
    rank = left_ref.shape[1]
    for g in range(left_ref.shape[0] // 8):
        left_ref[pl.ds(g * 8, 8), :] = left[:, g * rank : (g + 1) * rank]


def shift(block, hop):
    return lax.ppermute(block, "x", [(i, (i + hop) % NX) for i in range(NX)])


def swap(block, mask):
    return lax.ppermute(block, "x", [(i, i ^ mask) for i in range(NX)])


def after(value, *others):
    return lax.optimization_barrier((value, *others))[0]


def local(acts, grad_y, w_base, a_left, b_right, magnitude):
    rows, din = acts.shape
    width = grad_y.shape[1]
    rank = a_left.shape[1]
    tokens = rows * NZ
    wider = din + NX * rank
    spot = lax.axis_index("x").astype(jnp.int32).reshape(1)
    mags = magnitude.reshape(1, width)
    a_turned = a_left.T
    wide = lax.all_gather(w_base, "x")
    parts = (w_base, a_turned, b_right, grad_y)
    (pay,) = call(
        merge_body,
        [shape((NY, grad_y.shape[0] + 16, width))],
        2 * din * width * rank,
        *parts,
        far=(0, 1, 2, 3),
        scratch=[pltpu.VMEM(p.shape, p.dtype) for p in parts]
        + [pltpu.SemaphoreType.DMA((4,))],
        limit=60,
    )
    got = lax.all_to_all(pay, "din", 0, 0, tiled=True)
    (many,) = call(
        many_body,
        [shape((NZ, rows, din))],
        0,
        after(acts, pay),
        out_specs=[HBM],
        scratch=[pltpu.SemaphoreType.DMA((NZ,))],
    )
    scaled = call(
        scale_body,
        [shape((tokens + rank, width))] * NX,
        4 * tokens * width * NX,
        spot, got, mags, b_right,
    )
    blocks = [scaled[0]] + [shift(scaled[k], HOPS[k]) for k in range(1, NX)]
    whole = lax.all_to_all(after(many, got), "z", 0, 0, tiled=True).reshape(tokens, din)
    (wide,) = call(
        bring_body,
        [shape(wide.shape)],
        0,
        wide,
        far=(0,),
        scratch=[pltpu.SemaphoreType.DMA((NX,))],
        limit=4,
    )
    part, *sides = call(
        acts_body,
        [shape((tokens, wider))] + [shape((rank + 16, width))] * NX,
        4 * tokens * din * width * NX,
        spot, *blocks, wide, a_turned, whole,
        out_specs=[HBM] * (1 + NX),
        scratch=[
            pltpu.VMEM((tokens, wider), BF16),
            pltpu.VMEM((tokens, NX * rank), F32),
            pltpu.VMEM((NX, rank + 16, width), BF16),
            pltpu.SemaphoreType.DMA((1 + din // STEP,)),
            pltpu.SemaphoreType.DMA((NX,)),
        ],
        limit=16,
    )
    back = lax.all_to_all(part.reshape(NZ, rows, wider), "z", 0, 0, tiled=True)
    met = [sides[0]] + [shift(sides[k], NX - HOPS[k]) for k in range(1, NX)]
    summed, keep, send = call(
        sum_body,
        [shape((rows, din)), shape((16, width), F32), shape((16, width))],
        0,
        spot, back,
        scratch=[pltpu.VMEM((rows, NX * rank), F32)],
    )
    more = swap(send, 1)
    (pay,) = call(meet_body, [shape((NY, 16, width))], 0, *met)
    right = lax.all_to_all(after(pay, send), "din", 0, 0, tiled=True)
    own, send = call(
        pair_body, [shape((8, width), F32), shape((16, width))], 0, keep, more
    )
    grad_left, grad_right, grad_mag = call(
        last_body,
        [shape((rows, rank), F32), shape((rank // NY, width), F32), shape((1, width), F32)],
        0,
        own, swap(send, 3), right, mags,
    )
    return (summed, grad_left, grad_right, grad_mag.reshape(width))


def solution(mesh):
    fine = Mesh(mesh.devices.reshape(NY, NX, NZ, 2), ("din", "x", "z", "layer"))
    return jax.shard_map(
        local,
        mesh=fine,
        in_specs=(
            P(("layer", "x", "z"), "din"),
            P(("layer", "din"), ("x", "z")),
            P(("layer", "din"), ("x", "z")),
            P(("layer", "din"), None),
            P("layer", ("x", "z")),
            P(("layer", "x", "z")),
        ),
        out_specs=(
            P(("layer", "x", "z"), "din"),
            P(("layer", "din", "x", "z"), None),
            P(("layer", "din"), ("x", "z")),
            P(("layer", "x", "z")),
        ),
        check_vma=False,
    )
```

```python
import jax
import jax.numpy as jnp
from jax import lax
from jax.experimental import pallas as pl
from jax.experimental.pallas import tpu as pltpu
from jax.sharding import Mesh, PartitionSpec as P

F32 = jnp.float32
BF16 = jnp.bfloat16
NX, NY, NZ = 4, 8, 8
NT = (((1,), (1,)), ((), ()))
TN = (((0,), (0,)), ((), ()))
NN = (((1,), (0,)), ((), ()))
VMEM = pl.BlockSpec(memory_space=pltpu.VMEM)
SMEM = pl.BlockSpec(memory_space=pltpu.SMEM)
HBM = pl.BlockSpec(memory_space=pltpu.HBM)
MIB = 1024 * 1024
STEP = 512
HOPS = (0, 1, 3, 2)


def dot(a, b, dims):
    return lax.dot_general(a, b, dims, preferred_element_type=F32)


def shape(dims, dtype=BF16):
    return jax.ShapeDtypeStruct(dims, dtype)


def call(body, outs, flops, *args, far=(), scratch=(), out_specs=None, limit=16):
    moved = sum(a.size * a.dtype.itemsize for a in args)
    moved += sum(o.size * o.dtype.itemsize for o in outs)
    specs = [
        HBM if i in far else SMEM if a.dtype == jnp.int32 else VMEM
        for i, a in enumerate(args)
    ]
    return pl.pallas_call(
        body,
        out_shape=outs,
        in_specs=specs,
        out_specs=out_specs or [VMEM] * len(outs),
        scratch_shapes=scratch,
        compiler_params=pltpu.CompilerParams(vmem_limit_bytes=limit * MIB),
        cost_estimate=pl.CostEstimate(
            flops=flops, bytes_accessed=moved, transcendentals=0
        ),
    )(*args)


def fetch(pairs, sems):
    copies = [
        pltpu.make_async_copy(src, dst, sems.at[i]) for i, (src, dst) in enumerate(pairs)
    ]
    for copy in copies:
        copy.start()
    return copies


def two_rows(value, width):
    high = value.astype(BF16).astype(F32)
    row = lax.broadcasted_iota(jnp.int32, (16, width), 0)
    return jnp.where(row == 0, high, jnp.where(row == 1, value - high, 0.0)).astype(BF16)


def merge_body(
    w_hbm, at_hbm, b_hbm, g_hbm, acts_hbm, pay_ref, many_hbm, w_ref, at_ref, b_ref, g_ref, acts_ref, sems, more
):
    copies = fetch(
        (
            (acts_hbm, acts_ref),
            (w_hbm, w_ref),
            (at_hbm, at_ref),
            (b_hbm, b_ref),
            (g_hbm, g_ref),
        ),
        sems,
    )
    copies[0].wait()
    repeats = fetch([(acts_ref, many_hbm.at[z]) for z in range(NZ)], more)
    for copy in copies[1:]:
        copy.wait()
    din, width = w_ref.shape
    tokens = g_ref.shape[0]
    total = jnp.zeros((1, width), F32)
    for i in range(0, din, STEP):
        merged = w_ref[pl.ds(i, STEP), :].astype(F32) + dot(
            at_ref[:, pl.ds(i, STEP)], b_ref[...], TN
        )
        total += jnp.sum(merged * merged, axis=0, keepdims=True)
    tail = two_rows(total, width)
    for y in range(NY):
        pay_ref[y, pl.ds(0, tokens), :] = g_ref[...]
        pay_ref[y, pl.ds(tokens, 16), :] = tail
    for copy in repeats:
        copy.wait()


def scale_body(x_ref, got_ref, mag_ref, b_ref, *outs):
    tokens = got_ref.shape[1] - 16
    width = got_ref.shape[2]
    squares = jnp.zeros((16, width), F32)
    for y in range(NY):
        squares += got_ref[y, pl.ds(tokens, 16), :].astype(F32)
    squares = jnp.sum(squares, axis=0, keepdims=True)
    scale = mag_ref[...] / jnp.sqrt(squares)
    half = NY // NX
    for hop, out in zip(HOPS, outs):
        block = lax.rem(x_ref[0] + hop, NX)
        for h in range(half):
            out[pl.ds(h * tokens, tokens), :] = (
                got_ref[block * half + h, pl.ds(0, tokens), :].astype(F32) * scale
            ).astype(BF16)
        out[pl.ds(half * tokens, b_ref.shape[0]), :] = b_ref[...]


def bring_body(wide_hbm, out_ref, sems):
    for copy in fetch([(wide_hbm.at[k], out_ref.at[k]) for k in range(NX)], sems):
        copy.wait()


def source(x_ref, k):
    return lax.rem(x_ref[0] + NX - HOPS[k], NX)


def acts_body(
    x_ref, s0, s1, s2, s3, wide, at, whole, out_hbm, *rest
):
    side_hbm, (out, lefts, sides, out_sems, side_sems) = rest[:NX], rest[NX:]
    blocks = (s0, s1, s2, s3)
    tokens, din = whole.shape
    rank = at.shape[0]
    steps = din // STEP
    place = [source(x_ref, k) for k in range(NX)]
    low = jnp.zeros((tokens, NX * rank), F32)
    for s in blocks:
        b = s[pl.ds(tokens, rank), :]
        low += dot(s[pl.ds(0, tokens), :], jnp.concatenate([b] * NX, axis=0), NT)
    low = low.astype(BF16)
    sends = []

    def send(start, count):
        sends.append(
            pltpu.make_async_copy(
                out.at[:, pl.ds(start, count)],
                out_hbm.at[:, pl.ds(start, count)],
                out_sems.at[len(sends)],
            )
        )
        sends[-1].start()

    group = lax.div(lax.broadcasted_iota(jnp.int32, (8, NX * rank), 1), rank)
    each = din // NX
    rows = each // NZ
    for q in range(NX):
        left = dot(whole[:, pl.ds(q * each, each)], low, TN)
        for z in range(NZ):
            piece = jnp.zeros((8, NX * rank), F32)
            for g in range(rows // 8):
                first = z * rows + g * 8
                piece += jnp.where(group == g, left[first : first + 8], 0.0)
            lefts[pl.ds(z * rows + q * 8, 8), :] = piece
    out[:, pl.ds(din, NX * rank)] = lefts[...].astype(BF16)
    send(din, NX * rank)
    for i in range(steps):
        total = dot(low[:, :rank], at[:, pl.ds(i * STEP, STEP)], NN)
        for k, s in enumerate(blocks):
            total += dot(
                s[pl.ds(0, tokens), :], wide[place[k], pl.ds(i * STEP, STEP), :], NT
            )
        out[:, pl.ds(i * STEP, STEP)] = total.astype(BF16)
        send(i * STEP, STEP)
    down = dot(whole[...], at[...], NT).astype(BF16)
    for k, s in enumerate(blocks):
        scaled = s[pl.ds(0, tokens), :]
        outputs = dot(whole[...], wide[place[k]], NN) + dot(
            down, s[pl.ds(tokens, rank), :], NN
        )
        stat = jnp.sum(scaled.astype(F32) * outputs, axis=0, keepdims=True)
        sides[k, pl.ds(0, rank), :] = dot(down, scaled, TN).astype(BF16)
        sides[k, pl.ds(rank, 16), :] = two_rows(stat, stat.shape[1])
        sends.append(pltpu.make_async_copy(sides.at[k], side_hbm[k], side_sems.at[k]))
        sends[-1].start()
    for copy in sends:
        copy.wait()


def meet_body(r0, r1, r2, r3, pay_ref):
    rows, width = r0.shape
    total = sum(r[...].astype(F32) for r in (r0, r1, r2, r3))
    stat = jnp.sum(total[rows - 16 :], axis=0, keepdims=True)
    tail = two_rows(stat, width).astype(F32)[:8]
    each = (rows - 16) // NY
    for y in range(NY):
        pay_ref[y, :, :] = jnp.concatenate(
            [total[y * each : (y + 1) * each], tail], axis=0
        ).astype(BF16)


def sum_body(x_ref, got_ref, acts_ref, keep_ref, send_ref, lefts):
    din = acts_ref.shape[1]
    total = sum(got_ref[z].astype(F32) for z in range(NZ))
    acts_ref[...] = total[:, :din].astype(BF16)
    lefts[...] = total[:, din:]

    def block(mask):
        x = jnp.bitwise_xor(x_ref[0], mask)
        return lefts[pl.ds(pl.multiple_of(x * 8, 8), 8), :]

    keep_ref[...] = jnp.concatenate([block(0), block(3)], axis=0)
    send_ref[...] = jnp.concatenate([block(1), block(2)], axis=0).astype(BF16)


def pair_body(keep_ref, got_ref, own_ref, send_ref):
    total = keep_ref[...] + got_ref[...].astype(F32)
    own_ref[...] = total[:8]
    send_ref[...] = jnp.concatenate([total[8:], total[8:]], axis=0).astype(BF16)


def last_body(own_ref, more_ref, got_ref, mag_ref, left_ref, right_ref, mag_out):
    total = sum(got_ref[y].astype(F32) for y in range(NY))
    right_ref[...] = total[:8]
    mag_out[...] = (total[8:9] + total[9:10]) / mag_ref[...]
    left = own_ref[...] + more_ref[...].astype(F32)[:8]
    rank = left_ref.shape[1]
    for g in range(left_ref.shape[0] // 8):
        left_ref[pl.ds(g * 8, 8), :] = left[:, g * rank : (g + 1) * rank]


def shift(block, hop):
    return lax.ppermute(block, "x", [(i, (i + hop) % NX) for i in range(NX)])


def swap(block, mask):
    return lax.ppermute(block, "x", [(i, i ^ mask) for i in range(NX)])


def after(value, *others):
    return lax.optimization_barrier((value, *others))[0]


def local(acts, grad_y, w_base, a_left, b_right, magnitude):
    rows, din = acts.shape
    width = grad_y.shape[1]
    rank = a_left.shape[1]
    tokens = rows * NZ
    wider = din + NX * rank
    spot = lax.axis_index("x").astype(jnp.int32).reshape(1)
    mags = magnitude.reshape(1, width)
    a_turned = a_left.T
    wide = lax.all_gather(w_base, "x")
    parts = (w_base, a_turned, b_right, grad_y)
    pay, many = call(
        merge_body,
        [shape((NY, grad_y.shape[0] + 16, width)), shape((NZ, rows, din))],
        2 * din * width * rank,
        *parts, acts,
        far=(0, 1, 2, 3, 4),
        out_specs=[VMEM, HBM],
        scratch=[pltpu.VMEM(p.shape, p.dtype) for p in (*parts, acts)]
        + [pltpu.SemaphoreType.DMA((5,)), pltpu.SemaphoreType.DMA((NZ,))],
        limit=60,
    )
    got = lax.all_to_all(pay, "din", 0, 0, tiled=True)
    scaled = call(
        scale_body,
        [shape((tokens + rank, width))] * NX,
        4 * tokens * width * NX,
        spot, got, mags, b_right,
    )
    blocks = [scaled[0]] + [shift(scaled[k], HOPS[k]) for k in range(1, NX)]
    whole = lax.all_to_all(after(many, got), "z", 0, 0, tiled=True).reshape(tokens, din)
    (wide,) = call(
        bring_body,
        [shape(wide.shape)],
        0,
        wide,
        far=(0,),
        scratch=[pltpu.SemaphoreType.DMA((NX,))],
        limit=4,
    )
    part, *sides = call(
        acts_body,
        [shape((tokens, wider))] + [shape((rank + 16, width))] * NX,
        4 * tokens * din * width * NX,
        spot, *blocks, wide, a_turned, whole,
        out_specs=[HBM] * (1 + NX),
        scratch=[
            pltpu.VMEM((tokens, wider), BF16),
            pltpu.VMEM((tokens, NX * rank), F32),
            pltpu.VMEM((NX, rank + 16, width), BF16),
            pltpu.SemaphoreType.DMA((1 + din // STEP,)),
            pltpu.SemaphoreType.DMA((NX,)),
        ],
        limit=16,
    )
    back = lax.all_to_all(part.reshape(NZ, rows, wider), "z", 0, 0, tiled=True)
    met = [sides[0]] + [shift(sides[k], NX - HOPS[k]) for k in range(1, NX)]
    summed, keep, send = call(
        sum_body,
        [shape((rows, din)), shape((16, width), F32), shape((16, width))],
        0,
        spot, back,
        scratch=[pltpu.VMEM((rows, NX * rank), F32)],
    )
    more = swap(send, 1)
    (pay,) = call(meet_body, [shape((NY, 16, width))], 0, *met)
    right = lax.all_to_all(after(pay, send), "din", 0, 0, tiled=True)
    own, send = call(
        pair_body, [shape((8, width), F32), shape((16, width))], 0, keep, more
    )
    grad_left, grad_right, grad_mag = call(
        last_body,
        [shape((rows, rank), F32), shape((rank // NY, width), F32), shape((1, width), F32)],
        0,
        own, swap(send, 3), right, mags,
    )
    return (summed, grad_left, grad_right, grad_mag.reshape(width))


def solution(mesh):
    fine = Mesh(mesh.devices.reshape(NY, NX, NZ, 2), ("din", "x", "z", "layer"))
    return jax.shard_map(
        local,
        mesh=fine,
        in_specs=(
            P(("layer", "x", "z"), "din"),
            P(("layer", "din"), ("x", "z")),
            P(("layer", "din"), ("x", "z")),
            P(("layer", "din"), None),
            P("layer", ("x", "z")),
            P(("layer", "x", "z")),
        ),
        out_specs=(
            P(("layer", "x", "z"), "din"),
            P(("layer", "din", "x", "z"), None),
            P(("layer", "din"), ("x", "z")),
            P(("layer", "x", "z")),
        ),
        check_vma=False,
    )
```
